32 devices in a mesh: prow: 8 (over z, core), pcol: 4 (over y, x).
Axes of the slice: x: 2, y: 2, z: 4, core: 2. Of those that a mesh axis runs over, the one named last changes fastest.
Arguments:
- tiles: bfloat16 [4096, 128, 128], P(('prow', 'pcol')), may hold values from -6 to 6
- tile_pos: int32 [4096, 2], P(('prow', 'pcol')), may hold values from -1 to 255, as said below
- pivots: int32 [2, 256], replicated, may hold values from 0 to 255, each once within a row
- inverses: bfloat16 [2, 256, 256], replicated, may hold values from -0.0234375 to 0.0234375
Outputs:
- factored: bfloat16 [4096, 128, 128], P(('prow', 'pcol'))
The draws below stay inside these ranges and needn't reach their ends.
Inputs may be any that keep to these rules, and one draw needn't show every extreme that they name: `tile_pos`: slot s of device (p, q) (device index p * 4 + q, p along prow) holds a tile (I, J) with I % 8 == p and (J // 2) % 4 == q, or is empty; no tile is listed twice; every tile with I < 4 or J < 4 is listed; listed slots come before empty ones on each device; some device has all 128 slots listed.
All inputs are finite; a program needn't handle non-finite values.
Results may differ from the reference program's by a relative error of at most 0.0067.
Values may be sent and summed in bfloat16 or wider, within the bound.
A program may use at most 128 MiB of HBM per device.

```python
import math
import jax
import jax.numpy as jnp
from jax import lax

TILE = 128
PANEL = 256
ROW_TILES = 32
PAIRS = 32
SLOTS = 128
ORDER = 32768
N_PROW = 8
N_PCOL = 4


def draw_tile_pos(key, part):
    row_procs = N_PROW
    col_procs = N_PCOL
    count = row_procs * col_procs
    col_tiles = 2 * PAIRS
    cells = ROW_TILES * col_tiles
    device = jnp.arange(count, dtype=jnp.int32)
    proc_row = (device // col_procs)[:, None, None]
    proc_col = (device % col_procs)[:, None, None]
    local_i = jnp.arange(ROW_TILES, dtype=jnp.int32)[None, :, None]
    local_q = jnp.arange(col_tiles, dtype=jnp.int32)[None, None, :]
    glob_row = jnp.broadcast_to(proc_row + row_procs * local_i, (count, ROW_TILES, col_tiles)).reshape(count, cells)
    glob_col = jnp.broadcast_to(2 * (proc_col + col_procs * (local_q // 2)) + local_q % 2, (count, ROW_TILES, col_tiles)).reshape(count, cells)
    dense = (glob_row < 4) | (glob_col < 4)
    keys = jax.random.split(jax.random.fold_in(key, 11), count)
    ranks = jax.vmap(lambda k: jax.random.permutation(k, cells))(keys).astype(jnp.int32)
    priority = jnp.where(dense, -1, ranks)
    order = jnp.argsort(priority, axis=1, stable=True)[:, :SLOTS]
    dense_count = jnp.sum(dense.astype(jnp.int32), axis=1)
    room = SLOTS - dense_count
    extra = jax.random.randint(jax.random.fold_in(key, 12), (count,), 0, room + 1)
    chosen = jax.random.randint(jax.random.fold_in(key, 13), (), 0, count)
    extra = jnp.where(device == chosen, room, extra)
    live = jnp.arange(SLOTS, dtype=jnp.int32)[None, :] < (dense_count + extra)[:, None]
    rows = jnp.take_along_axis(glob_row, order, axis=1)
    cols = jnp.take_along_axis(glob_col, order, axis=1)
    rows = jnp.where(live, rows, -1)
    cols = jnp.where(live, cols, -1)
    return jnp.stack([rows, cols], axis=-1).reshape(count * SLOTS, 2).astype(jnp.int32)


def shard_levels(own_key, dims, pieces, least, largest):
    loudness = 1.0
    for axis_at, blocks in pieces:
        draws = jax.random.uniform(jax.random.fold_in(jax.random.fold_in(own_key, 6), axis_at), (blocks,), jnp.float32, least / len(pieces), largest / len(pieces))
        loudness = loudness * jnp.repeat(jnp.exp(draws), dims[axis_at] // blocks).reshape((-1,) + (1,) * (len(dims) - 1 - axis_at))
    return loudness


def centred(stream_key, shape, width, reach, cuts=(), kind=jnp.bfloat16):
    entries = jax.random.normal(stream_key, shape, jnp.float32) * width
    if len(cuts) > 0:
        entries = shard_levels(stream_key, shape, cuts, -0.22, 0.18) * entries
    return jnp.clip(entries, min=-reach, max=reach).astype(kind)


def setup_inputs(seed: int = 0) -> dict:
    key_list = jax.random.split(jax.random.key(seed), 5)
    tiles = centred(key_list[0], (N_PROW * N_PCOL * SLOTS, TILE, TILE), 1.0, 6.0, ((0, 32),))
    tile_pos = draw_tile_pos(jax.random.fold_in(key_list[4], 71), 0)
    pivots = jax.vmap(lambda own: jax.random.permutation(own, PANEL))(jax.random.split(key_list[2], 2)).reshape((2, PANEL)).astype(jnp.int32)
    inverses = centred(key_list[3], (2, PANEL, PANEL), (PANEL * PANEL) ** -0.5, 0.0234375)
    return {"tiles": tiles, "tile_pos": tile_pos, "pivots": pivots, "inverses": inverses}


def panel_step(current, tile_row, tile_col, order, inverse, first, tiles_n):
    edge = current.shape[1]
    in_column = (tile_col >= first) & (tile_col < first + 2)
    col_keys = jnp.where(in_column, tile_row * 2 + tile_col - first, 2 * tiles_n).astype(jnp.int32)
    column = jnp.zeros((2 * tiles_n, edge, edge), current.dtype).at[col_keys].set(current, mode="drop")
    column = column.reshape(tiles_n, 2, edge, edge).transpose(0, 2, 1, 3).reshape(tiles_n * edge, 2 * edge)
    lower = jnp.dot(column, inverse, preferred_element_type=jnp.float32).astype(jnp.bfloat16)
    in_block = (tile_row >= first) & (tile_row < first + 2)
    row_keys = jnp.where(in_block, (tile_row - first) * tiles_n + tile_col, 2 * tiles_n).astype(jnp.int32)
    rows = jnp.zeros((2 * tiles_n, edge, edge), current.dtype).at[row_keys].set(current, mode="drop")
    rows = rows.reshape(2, tiles_n, edge, edge).transpose(0, 2, 1, 3).reshape(2 * edge, tiles_n * edge)
    upper = rows[order]
    lower_tiles = lower.reshape(tiles_n, edge, 2 * edge)
    upper_tiles = upper.reshape(2 * edge, tiles_n, edge).transpose(1, 0, 2)
    lower_parts = lower_tiles.reshape(tiles_n, edge, 2, edge).transpose(0, 2, 1, 3)
    upper_parts = upper_tiles.reshape(tiles_n, 2, edge, edge)
    total = current.shape[0]
    blk = math.gcd(total, 256)
    count = total // blk

    def one_block(args):
        cur, rws, cls = args
        safe_row = jnp.clip(rws, 0, tiles_n - 1)
        safe_col = jnp.clip(cls, 0, tiles_n - 1)
        left = lower_tiles[safe_row].astype(jnp.float32)
        right = upper_tiles[safe_col].astype(jnp.float32)
        product = jnp.einsum("sik,skj->sij", left, right, precision=lax.Precision.HIGHEST)
        updated = (cur.astype(jnp.float32) - product).astype(jnp.bfloat16)
        trailing = (rws >= first + 2) & (cls >= first + 2)
        is_lower = (cls >= first) & (cls < first + 2) & (rws >= first + 2)
        is_upper = (rws >= first) & (rws < first + 2)
        lower_write = lower_parts[safe_row, jnp.clip(cls - first, 0, 1)]
        upper_write = upper_parts[safe_col, jnp.clip(rws - first, 0, 1)]
        out = jnp.where(trailing[:, None, None], updated, cur)
        out = jnp.where(is_lower[:, None, None], lower_write, out)
        out = jnp.where(is_upper[:, None, None], upper_write, out)
        return out

    result = lax.map(one_block, (current.reshape(count, blk, edge, edge), tile_row.reshape(count, blk), tile_col.reshape(count, blk)))
    return result.reshape(current.shape)


def reference(tiles, tile_pos, pivots, inverses):
    tiles_n = ORDER // TILE
    tile_row = tile_pos[:, 0]
    tile_col = tile_pos[:, 1]
    current = tiles
    for panel in range(2):
        current = panel_step(current, tile_row, tile_col, pivots[panel], inverses[panel], 2 * panel, tiles_n)
    return current
```

```python
import functools
import jax
import jax.numpy as jnp
from jax import lax
from jax.experimental import pallas as pl
from jax.experimental.pallas import tpu as pltpu
from jax.sharding import PartitionSpec as P

ROW_TILES = 32
CHUNKS = 16
GROUP = 8
MESH = pl.DeviceIdType.MESH


def slot_lookup(keys, count):
    targets = jnp.arange(count, dtype=jnp.int32)
    matches = keys[None, :] == targets[:, None]
    positions = jnp.arange(keys.shape[0], dtype=jnp.int32)
    return jnp.sum(jnp.where(matches, positions[None, :], 0), axis=1)


def exchange(
    nz, nbits, cols,
    slot_r, slot_l, tiles,
    rows, side, ext_r, ext_c,
    up_send, down_send, sib_send, z_recv, sib_recv,
    l_send, l_recv, e_sem, f_send, f_recv,
):
    p = lax.axis_index("prow")
    v = lax.axis_index("pcol")
    z = p // 2
    core = p % 2
    other = p + 1 - 2 * core
    cw = cols // CHUNKS
    rw = ROW_TILES // CHUNKS
    n = CHUNKS

    def flip(b):
        return v + b - 2 * b * ((v // b) % 2)

    barrier = pltpu.get_barrier_semaphore()

    @pl.when(z > 0)
    def _():
        pl.semaphore_signal(barrier, inc=1, device_id={"prow": p - 2, "pcol": v}, device_id_type=MESH)

    @pl.when(z < nz - 1)
    def _():
        pl.semaphore_signal(barrier, inc=1, device_id={"prow": p + 2, "pcol": v}, device_id_type=MESH)

    pl.semaphore_signal(barrier, inc=1, device_id={"prow": other, "pcol": v}, device_id_type=MESH)
    for bi in range(nbits):
        pl.semaphore_signal(barrier, inc=1, device_id={"prow": p, "pcol": flip(1 << bi)}, device_id_type=MESH)

    @pl.when(z < 2)
    def _():
        @pl.loop(0, cols)
        def _(c):
            rows[c, p] = tiles[slot_r[c]]

    @pl.when(v < 2)
    def _():
        @pl.loop(0, ROW_TILES)
        def _(i):
            side[v, i, 0] = tiles[slot_l[2 * i]]
            side[v, i, 1] = tiles[slot_l[2 * i + 1]]

    ends = (z == 0).astype(jnp.int32) + (z == nz - 1).astype(jnp.int32)
    pl.semaphore_wait(barrier, 3 + nbits - ends)

    def block(k, j):
        return rows.at[pl.ds(j * cw, cw), 2 * k + core]

    def up(k, j):
        return pltpu.make_async_remote_copy(
            block(k, j), block(k, j), up_send.at[k, j], z_recv.at[k, j],
            device_id={"prow": p + 2, "pcol": v}, device_id_type=MESH)

    def down(k, j):
        return pltpu.make_async_remote_copy(
            block(k, j), block(k, j), down_send.at[k, j], z_recv.at[k, j],
            device_id={"prow": p - 2, "pcol": v}, device_id_type=MESH)

    def sib(k, j):
        return pltpu.make_async_remote_copy(
            block(k, j), block(k, j), sib_send.at[k, j], sib_recv.at[k, j],
            device_id={"prow": other, "pcol": v}, device_id_type=MESH)

    def sib_in(k, j):
        there = rows.at[pl.ds(j * cw, cw), 2 * k + 1 - core]
        return pltpu.make_async_remote_copy(
            there, there, sib_send.at[k, j], sib_recv.at[k, j],
            device_id={"prow": other, "pcol": v}, device_id_type=MESH)

    def goes_up(k):
        return jnp.logical_and(z >= k, z < nz - 1)

    def goes_down(k):
        return jnp.logical_and(z <= k, z > 0)

    def forward(k, j):
        @pl.when(goes_up(k))
        def _():
            up(k, j).start()

        @pl.when(goes_down(k))
        def _():
            down(k, j).start()

        sib(k, j).start()

    def own(k, j):
        @pl.when(z == k)
        def _():
            forward(k, j)

    def label(s):
        return v if s == 0 else v + 1 - 2 * (v % 2)

    def side_copy(s, j, bi):
        part = side.at[s, pl.ds(j * rw, rw)]
        return pltpu.make_async_remote_copy(
            part, part, l_send.at[s, bi, j], l_recv.at[s, j],
            device_id={"prow": p, "pcol": flip(1 << bi)}, device_id_type=MESH)

    def side_forward(s, j):
        for bi in range(nbits):
            @pl.when(label(s) % (2 << bi) == 0)
            def _():
                side_copy(s, j, bi).start()

    def ext_copy(source, sem, target, recv):
        return pltpu.make_async_remote_copy(
            source, ext_r.at[core], e_sem.at[sem], e_sem.at[recv],
            device_id={"prow": target, "pcol": v}, device_id_type=MESH)

    def ext_forward(source):
        @pl.when(goes_up(1))
        def _():
            ext_copy(source, 0, p + 2, 3).start()

        @pl.when(goes_down(1))
        def _():
            ext_copy(source, 1, p - 2, 3).start()

        ext_copy(source, 2, other, 4).start()

    def corner_copy(source, bi):
        return pltpu.make_async_remote_copy(
            source, ext_c, f_send.at[bi], f_recv.at[0],
            device_id={"prow": p, "pcol": flip(1 << bi)}, device_id_type=MESH)

    def corner_forward(source):
        for bi in range(nbits):
            @pl.when(label(1) % (2 << bi) == 0)
            def _():
                corner_copy(source, bi).start()

    for k in range(2):
        own(k, 0)
        own(k, 1)

    @pl.loop(0, n)
    def _(j):
        @pl.when(j + 2 < n)
        def _():
            own(0, j + 2)
            own(1, j + 2)

        @pl.when(j < n // 2)
        def _():
            for h in range(2):
                for s in range(2):
                    @pl.when(v == s)
                    def _():
                        side_forward(s, 2 * j + h)

        for k in (1, 0):
            @pl.when(z != k)
            def _():
                up(k, j).wait_recv()
                forward(k, j)

        @pl.when(j < n // 2)
        def _():
            for h in range(2):
                for s in range(2):
                    @pl.when(v != s)
                    def _():
                        side_copy(s, 2 * j + h, 0).wait_recv()
                        side_forward(s, 2 * j + h)

        @pl.when(jnp.logical_and(j == 0, z == 1))
        def _():
            ext_forward(side.at[0, 0])
            ext_r[core] = side[0, 0]

        @pl.when(jnp.logical_and(j == 2, z != 1))
        def _():
            ext_copy(ext_r.at[core], 0, other, 3).wait_recv()
            ext_forward(ext_r.at[core])

        @pl.when(j == 2)
        def _():
            sib_in(0, 0).wait_recv()

            @pl.when(v == 1)
            def _():
                corner_forward(rows.at[pl.ds(0, 2), pl.ds(0, 2)])
                ext_c[...] = rows[pl.ds(0, 2), pl.ds(0, 2)]

        @pl.when(jnp.logical_and(j == 4, v != 1))
        def _():
            corner_copy(ext_c, 0).wait_recv()
            corner_forward(ext_c)

    @pl.loop(0, n)
    def _(j):
        for k in range(2):
            @pl.when(goes_up(k))
            def _():
                up(k, j).wait_send()

            @pl.when(goes_down(k))
            def _():
                down(k, j).wait_send()

            sib(k, j).wait_send()

        sib_in(1, j).wait_recv()

        @pl.when(j > 0)
        def _():
            sib_in(0, j).wait_recv()

        for s in range(2):
            for bi in range(nbits):
                @pl.when(label(s) % (2 << bi) == 0)
                def _():
                    side_copy(s, j, bi).wait_send()

    @pl.when(goes_up(1))
    def _():
        ext_copy(ext_r.at[core], 0, other, 3).wait_send()

    @pl.when(goes_down(1))
    def _():
        ext_copy(ext_r.at[core], 1, other, 3).wait_send()

    ext_copy(ext_r.at[core], 2, other, 4).wait_send()
    pltpu.make_async_remote_copy(
        ext_r.at[core], ext_r.at[1 - core], e_sem.at[2], e_sem.at[4],
        device_id={"prow": other, "pcol": v}, device_id_type=MESH).wait_recv()
    for bi in range(nbits):
        @pl.when(label(1) % (2 << bi) == 0)
        def _():
            corner_copy(ext_c, bi).wait_send()


def dot(a, b):
    return jnp.dot(a, b, preferred_element_type=jnp.float32)


def update(
    cols, place,
    order, inverse, rows, side, ext_r, ext_c, tiles,
    out,
    m0, m1, r1, final,
):
    p = lax.axis_index("prow")
    v = lax.axis_index("pcol")
    bf = jnp.bfloat16
    spread = lax.broadcasted_iota(jnp.int32, (256, 256), 1)
    perm0 = (order[0] == spread).astype(bf)
    perm1 = (order[1] == spread).astype(bf)
    inv0, inv1 = inverse[0], inverse[1]
    mix0 = dot(inv0, perm0).astype(bf)
    mix1 = dot(inv1, perm1).astype(bf)
    corner = jnp.concatenate(
        [jnp.concatenate([ext_c[0, r], ext_c[1, r]], axis=1) for r in range(2)], axis=0)
    pivot_rows = jnp.concatenate(
        [jnp.concatenate([ext_r[r, 0], ext_r[r, 1]], axis=1) for r in range(2)], axis=0)
    step = 4

    @pl.loop(0, ROW_TILES, step=step)
    def _(i):
        def wide(s):
            return jnp.concatenate(
                [side[s, pl.ds(i, step), h].reshape(step * 128, 128) for h in range(2)], axis=1)

        left = wide(0)
        lower = dot(left, mix0).astype(bf)
        m0[pl.ds(i, step)] = lower.reshape(step, 128, 256)
        right = (wide(1).astype(jnp.float32) - dot(lower, corner)).astype(bf)
        m1[pl.ds(i, step)] = dot(right, mix1).astype(bf).reshape(step, 128, 256)

        def keep(value):
            for u in range(step):
                for h in range(2):
                    final[cols + 2 * (i + u) + h] = value[u * 128:(u + 1) * 128, h * 128:(h + 1) * 128]

        @pl.when(v == 0)
        def _():
            keep(dot(left, inv0).astype(bf))

        @pl.when(v == 1)
        def _():
            keep(dot(right, inv1).astype(bf))

    lead = dot(pivot_rows, mix0).astype(bf)

    @pl.loop(0, cols, step=step)
    def _(c):
        top = jnp.concatenate([rows[c + u, pl.ds(0, 2)].reshape(256, 128) for u in range(step)], axis=1)
        low = jnp.concatenate([rows[c + u, pl.ds(2, 2)].reshape(256, 128) for u in range(step)], axis=1)
        value = (low.astype(jnp.float32) - dot(lead, top)).astype(bf)
        for u in range(step):
            r1[c + u] = value[:, u * 128:(u + 1) * 128]

    @pl.when(v == 0)
    def _():
        value = dot(pivot_rows, inv0).astype(bf)
        r1[0] = value[:, :128]
        r1[1] = value[:, 128:]

    narrow = lax.broadcasted_iota(jnp.int32, (128, 256), 1)

    @pl.when(p < 2)
    def _():
        part = (order[0, pl.ds(p * 128, 128)] == narrow).astype(bf)

        @pl.loop(0, cols, step=step)
        def _(c):
            top = jnp.concatenate([rows[c + u, pl.ds(0, 2)].reshape(256, 128) for u in range(step)], axis=1)
            value = dot(part, top).astype(bf)
            for u in range(step):
                final[c + u] = value[:, u * 128:(u + 1) * 128]

    @pl.when(jnp.logical_and(p >= 2, p < 4))
    def _():
        part = (order[1, pl.ds((p - 2) * 128, 128)] == narrow).astype(bf)

        @pl.loop(0, cols, step=step)
        def _(c):
            low = jnp.concatenate([r1[c + u] for u in range(step)], axis=1)
            value = dot(part, low).astype(bf)
            for u in range(step):
                final[c + u] = value[:, u * 128:(u + 1) * 128]

    slots = tiles.shape[0]

    @pl.loop(0, slots, step=GROUP)
    def _(base):
        for u in range(GROUP):
            s = base + u
            i, c, f, kind = place[0, s], place[1, s], place[2, s], place[3, s]
            old = tiles[s].astype(jnp.float32)
            total = dot(m0[i], rows[c, pl.ds(0, 2)].reshape(256, 128)) + dot(m1[i], r1[c])
            other = jnp.where(kind == 1, final[f].astype(jnp.float32), old)
            out[s] = jnp.where(kind == 0, old - total, other).astype(bf)


def local(tiles, tile_pos, pivots, inverses):
    slots, edge, _ = tiles.shape
    row_procs = lax.axis_size("prow")
    col_procs = lax.axis_size("pcol")
    nz = row_procs // 2
    nbits = col_procs.bit_length() - 1
    cols = ROW_TILES * row_procs // col_procs
    tile_row = tile_pos[:, 0]
    tile_col = tile_pos[:, 1]
    local_row = jnp.clip(tile_row // row_procs, 0, ROW_TILES - 1)
    local_col = jnp.clip(2 * (tile_col // 2 // col_procs) + tile_col % 2, 0, cols - 1)
    listed = tile_row >= 0
    is_upper = listed & (tile_row < 4)
    is_side = listed & (tile_col < 4)
    side_key = local_row * 2 + tile_col % 2
    slot_r = slot_lookup(jnp.where(is_upper, local_col, -1), cols)
    slot_l = slot_lookup(jnp.where(is_side, side_key, -1), 2 * ROW_TILES)
    done = jnp.where(is_upper, local_col, cols + side_key)
    kind = jnp.where(listed, jnp.where(is_upper | is_side, 1, 0), 2)
    done = jnp.where(kind == 1, done, 0)
    place = jnp.stack([local_row, local_col, done, kind]).astype(jnp.int32)

    bf = jnp.bfloat16
    smem = pl.BlockSpec(memory_space=pltpu.SMEM)
    vmem = pl.BlockSpec(memory_space=pltpu.VMEM)
    dma = pltpu.SemaphoreType.DMA
    n = CHUNKS
    rows, side, ext_r, ext_c = pl.pallas_call(
        functools.partial(exchange, nz, nbits, cols),
        out_shape=[
            jax.ShapeDtypeStruct((cols, 4, edge, edge), bf),
            jax.ShapeDtypeStruct((2, ROW_TILES, 2, edge, edge), bf),
            jax.ShapeDtypeStruct((2, 2, edge, edge), bf),
            jax.ShapeDtypeStruct((2, 2, edge, edge), bf),
        ],
        in_specs=[smem, smem, vmem],
        out_specs=[vmem] * 4,
        scratch_shapes=[
            dma((2, n)), dma((2, n)), dma((2, n)), dma((2, n)), dma((2, n)),
            dma((2, nbits, n)), dma((2, n)), dma((5,)), dma((nbits,)), dma((1,)),
        ],
        compiler_params=pltpu.CompilerParams(
            collective_id=0, has_side_effects=True, vmem_limit_bytes=40 * 1024 * 1024),
        name="exchange",
    )(slot_r, slot_l, tiles)
    return pl.pallas_call(
        functools.partial(update, cols),
        out_shape=jax.ShapeDtypeStruct(tiles.shape, bf),
        in_specs=[smem] + [vmem] * 7,
        out_specs=vmem,
        scratch_shapes=[
            pltpu.VMEM((ROW_TILES, edge, 2 * edge), bf),
            pltpu.VMEM((ROW_TILES, edge, 2 * edge), bf),
            pltpu.VMEM((cols, 2 * edge, edge), bf),
            pltpu.VMEM((cols + 2 * ROW_TILES, edge, edge), bf),
        ],
        compiler_params=pltpu.CompilerParams(vmem_limit_bytes=48 * 1024 * 1024),
        name="update",
    )(place, pivots.reshape(2, 2 * edge, 1), inverses, rows, side, ext_r, ext_c, tiles)


def solution(mesh):
    return jax.shard_map(
        local,
        mesh=mesh,
        in_specs=(P(("prow", "pcol"), None, None), P(("prow", "pcol"), None), P(), P()),
        out_specs=P(("prow", "pcol"), None, None),
        check_vma=False,
    )
```

```python
import functools
import jax
import jax.numpy as jnp
from jax import lax
from jax.experimental import pallas as pl
from jax.experimental.pallas import tpu as pltpu
from jax.sharding import PartitionSpec as P

ROW_TILES = 32
CHUNKS = 16
GROUP = 8
MESH = pl.DeviceIdType.MESH


def slot_lookup(keys, count):
    targets = jnp.arange(count, dtype=jnp.int32)
    matches = keys[None, :] == targets[:, None]
    positions = jnp.arange(keys.shape[0], dtype=jnp.int32)
    return jnp.sum(jnp.where(matches, positions[None, :], 0), axis=1)


def exchange(
    nz, nbits, cols,
    slot_r, slot_l, tiles,
    rows, side, ext_r, ext_c,
    up_send, down_send, sib_send, z_recv, sib_recv,
    l_send, l_recv, e_sem, f_send, f_recv,
):
    p = lax.axis_index("prow")
    v = lax.axis_index("pcol")
    z = p // 2
    core = p % 2
    other = p + 1 - 2 * core
    cw = cols // CHUNKS
    rw = ROW_TILES // CHUNKS
    n = CHUNKS

    def flip(b):
        return v + b - 2 * b * ((v // b) % 2)

    barrier = pltpu.get_barrier_semaphore()

    @pl.when(z > 0)
    def _():
        pl.semaphore_signal(barrier, inc=1, device_id={"prow": p - 2, "pcol": v}, device_id_type=MESH)

    @pl.when(z < nz - 1)
    def _():
        pl.semaphore_signal(barrier, inc=1, device_id={"prow": p + 2, "pcol": v}, device_id_type=MESH)

    pl.semaphore_signal(barrier, inc=1, device_id={"prow": other, "pcol": v}, device_id_type=MESH)
    for bi in range(nbits):
        pl.semaphore_signal(barrier, inc=1, device_id={"prow": p, "pcol": flip(1 << bi)}, device_id_type=MESH)

    @pl.when(z < 2)
    def _():
        @pl.loop(0, cols)
        def _(c):
            rows[c, p] = tiles[slot_r[c]]

    @pl.when(v < 2)
    def _():
        @pl.loop(0, ROW_TILES)
        def _(i):
            side[v, i, 0] = tiles[slot_l[2 * i]]
            side[v, i, 1] = tiles[slot_l[2 * i + 1]]

    ends = (z == 0).astype(jnp.int32) + (z == nz - 1).astype(jnp.int32)
    pl.semaphore_wait(barrier, 3 + nbits - ends)

    def block(k, j):
        return rows.at[pl.ds(j * cw, cw), 2 * k + core]

    def up(k, j):
        return pltpu.make_async_remote_copy(
            block(k, j), block(k, j), up_send.at[k, j], z_recv.at[k, j],
            device_id={"prow": p + 2, "pcol": v}, device_id_type=MESH)

    def down(k, j):
        return pltpu.make_async_remote_copy(
            block(k, j), block(k, j), down_send.at[k, j], z_recv.at[k, j],
            device_id={"prow": p - 2, "pcol": v}, device_id_type=MESH)

    def sib(k, j):
        return pltpu.make_async_remote_copy(
            block(k, j), block(k, j), sib_send.at[k, j], sib_recv.at[k, j],
            device_id={"prow": other, "pcol": v}, device_id_type=MESH)

    def sib_in(k, j):
        there = rows.at[pl.ds(j * cw, cw), 2 * k + 1 - core]
        return pltpu.make_async_remote_copy(
            there, there, sib_send.at[k, j], sib_recv.at[k, j],
            device_id={"prow": other, "pcol": v}, device_id_type=MESH)

    def goes_up(k):
        return jnp.logical_and(z >= k, z < nz - 1)

    def goes_down(k):
        return jnp.logical_and(z <= k, z > 0)

    def forward(k, j):
        @pl.when(goes_up(k))
        def _():
            up(k, j).start()

        @pl.when(goes_down(k))
        def _():
            down(k, j).start()

        sib(k, j).start()

    def own(k, j):
        @pl.when(z == k)
        def _():
            forward(k, j)

    def label(s):
        return v if s == 0 else v + 1 - 2 * (v % 2)

    def side_copy(s, j, bi):
        part = side.at[s, pl.ds(j * rw, rw)]
        return pltpu.make_async_remote_copy(
            part, part, l_send.at[s, bi, j], l_recv.at[s, j],
            device_id={"prow": p, "pcol": flip(1 << bi)}, device_id_type=MESH)

    def side_forward(s, j):
        for bi in range(nbits):
            @pl.when(label(s) % (2 << bi) == 0)
            def _():
                side_copy(s, j, bi).start()

    def ext_copy(source, sem, target, recv):
        return pltpu.make_async_remote_copy(
            source, ext_r.at[core], e_sem.at[sem], e_sem.at[recv],
            device_id={"prow": target, "pcol": v}, device_id_type=MESH)

    def ext_forward(source):
        @pl.when(goes_up(1))
        def _():
            ext_copy(source, 0, p + 2, 3).start()

        @pl.when(goes_down(1))
        def _():
            ext_copy(source, 1, p - 2, 3).start()

        ext_copy(source, 2, other, 4).start()

    def corner_copy(source, bi):
        return pltpu.make_async_remote_copy(
            source, ext_c, f_send.at[bi], f_recv.at[0],
            device_id={"prow": p, "pcol": flip(1 << bi)}, device_id_type=MESH)

    def corner_forward(source):
        for bi in range(nbits):
            @pl.when(label(1) % (2 << bi) == 0)
            def _():
                corner_copy(source, bi).start()

    def side_turn(s, j):
        depth = sum((label(s) // (1 << bi)) % 2 for bi in range(nbits))
        at = j - 2 * depth + 1

        @pl.when(jnp.logical_and(depth > 0, jnp.logical_and(at >= 0, at < n)))
        def _():
            side_copy(s, at, 0).wait_recv()
            side_forward(s, at)

    for k in range(2):
        own(k, 0)
        own(k, 1)

    @pl.loop(0, n)
    def _(j):
        @pl.when(j + 2 < n)
        def _():
            own(0, j + 2)
            own(1, j + 2)

        for s in range(2):
            @pl.when(v == s)
            def _():
                side_forward(s, j)

        for k in (1, 0):
            @pl.when(z != k)
            def _():
                up(k, j).wait_recv()
                forward(k, j)

        for s in range(2):
            side_turn(s, j)

        @pl.when(jnp.logical_and(j == 2 * nbits, z == 1))
        def _():
            ext_forward(side.at[0, 0])
            ext_r[core] = side[0, 0]

        @pl.when(jnp.logical_and(j == 2 * nbits + 1, z != 1))
        def _():
            ext_copy(ext_r.at[core], 0, other, 3).wait_recv()
            ext_forward(ext_r.at[core])

        @pl.when(j == 2)
        def _():
            sib_in(0, 0).wait_recv()

            @pl.when(v == 1)
            def _():
                corner_forward(rows.at[pl.ds(0, 2), pl.ds(0, 2)])
                ext_c[...] = rows[pl.ds(0, 2), pl.ds(0, 2)]

        @pl.when(jnp.logical_and(j == 4, v != 1))
        def _():
            corner_copy(ext_c, 0).wait_recv()
            corner_forward(ext_c)

    @pl.loop(n, n + 2 * nbits)
    def _(j):
        for s in range(2):
            side_turn(s, j)

    @pl.loop(0, n)
    def _(j):
        for k in range(2):
            @pl.when(goes_up(k))
            def _():
                up(k, j).wait_send()

            @pl.when(goes_down(k))
            def _():
                down(k, j).wait_send()

            sib(k, j).wait_send()

        sib_in(1, j).wait_recv()

        @pl.when(j > 0)
        def _():
            sib_in(0, j).wait_recv()

        for s in range(2):
            for bi in range(nbits):
                @pl.when(label(s) % (2 << bi) == 0)
                def _():
                    side_copy(s, j, bi).wait_send()

    @pl.when(goes_up(1))
    def _():
        ext_copy(ext_r.at[core], 0, other, 3).wait_send()

    @pl.when(goes_down(1))
    def _():
        ext_copy(ext_r.at[core], 1, other, 3).wait_send()

    ext_copy(ext_r.at[core], 2, other, 4).wait_send()
    pltpu.make_async_remote_copy(
        ext_r.at[core], ext_r.at[1 - core], e_sem.at[2], e_sem.at[4],
        device_id={"prow": other, "pcol": v}, device_id_type=MESH).wait_recv()
    for bi in range(nbits):
        @pl.when(label(1) % (2 << bi) == 0)
        def _():
            corner_copy(ext_c, bi).wait_send()


def dot(a, b):
    return jnp.dot(a, b, preferred_element_type=jnp.float32)


def update(
    cols, place,
    order, inverse, rows, side, ext_r, ext_c, tiles,
    out,
    m0, m1, r1, final,
):
    p = lax.axis_index("prow")
    v = lax.axis_index("pcol")
    bf = jnp.bfloat16
    spread = lax.broadcasted_iota(jnp.int32, (256, 256), 1)
    perm0 = (order[0] == spread).astype(bf)
    perm1 = (order[1] == spread).astype(bf)
    inv0, inv1 = inverse[0], inverse[1]
    mix0 = dot(inv0, perm0).astype(bf)
    mix1 = dot(inv1, perm1).astype(bf)
    corner = jnp.concatenate(
        [jnp.concatenate([ext_c[0, r], ext_c[1, r]], axis=1) for r in range(2)], axis=0)
    pivot_rows = jnp.concatenate(
        [jnp.concatenate([ext_r[r, 0], ext_r[r, 1]], axis=1) for r in range(2)], axis=0)
    step = 4

    @pl.loop(0, ROW_TILES, step=step)
    def _(i):
        def wide(s):
            return jnp.concatenate(
                [side[s, pl.ds(i, step), h].reshape(step * 128, 128) for h in range(2)], axis=1)

        left = wide(0)
        lower = dot(left, mix0).astype(bf)
        m0[pl.ds(i, step)] = lower.reshape(step, 128, 256)
        right = (wide(1).astype(jnp.float32) - dot(lower, corner)).astype(bf)
        m1[pl.ds(i, step)] = dot(right, mix1).astype(bf).reshape(step, 128, 256)

        def keep(value):
            for u in range(step):
                for h in range(2):
                    final[cols + 2 * (i + u) + h] = value[u * 128:(u + 1) * 128, h * 128:(h + 1) * 128]

        @pl.when(v == 0)
        def _():
            keep(dot(left, inv0).astype(bf))

        @pl.when(v == 1)
        def _():
            keep(dot(right, inv1).astype(bf))

    lead = dot(pivot_rows, mix0).astype(bf)

    @pl.loop(0, cols, step=step)
    def _(c):
        top = jnp.concatenate([rows[c + u, pl.ds(0, 2)].reshape(256, 128) for u in range(step)], axis=1)
        low = jnp.concatenate([rows[c + u, pl.ds(2, 2)].reshape(256, 128) for u in range(step)], axis=1)
        value = (low.astype(jnp.float32) - dot(lead, top)).astype(bf)
        for u in range(step):
            r1[c + u] = value[:, u * 128:(u + 1) * 128]

    @pl.when(v == 0)
    def _():
        value = dot(pivot_rows, inv0).astype(bf)
        r1[0] = value[:, :128]
        r1[1] = value[:, 128:]

    narrow = lax.broadcasted_iota(jnp.int32, (128, 256), 1)

    @pl.when(p < 2)
    def _():
        part = (order[0, pl.ds(p * 128, 128)] == narrow).astype(bf)

        @pl.loop(0, cols, step=step)
        def _(c):
            top = jnp.concatenate([rows[c + u, pl.ds(0, 2)].reshape(256, 128) for u in range(step)], axis=1)
            value = dot(part, top).astype(bf)
            for u in range(step):
                final[c + u] = value[:, u * 128:(u + 1) * 128]

    @pl.when(jnp.logical_and(p >= 2, p < 4))
    def _():
        part = (order[1, pl.ds((p - 2) * 128, 128)] == narrow).astype(bf)

        @pl.loop(0, cols, step=step)
        def _(c):
            low = jnp.concatenate([r1[c + u] for u in range(step)], axis=1)
            value = dot(part, low).astype(bf)
            for u in range(step):
                final[c + u] = value[:, u * 128:(u + 1) * 128]

    slots = tiles.shape[0]

    @pl.loop(0, slots, step=GROUP)
    def _(base):
        for u in range(GROUP):
            s = base + u
            i, c, f, kind = place[0, s], place[1, s], place[2, s], place[3, s]
            old = tiles[s].astype(jnp.float32)
            total = dot(m0[i], rows[c, pl.ds(0, 2)].reshape(256, 128)) + dot(m1[i], r1[c])
            other = jnp.where(kind == 1, final[f].astype(jnp.float32), old)
            out[s] = jnp.where(kind == 0, old - total, other).astype(bf)


def local(tiles, tile_pos, pivots, inverses):
    slots, edge, _ = tiles.shape
    row_procs = lax.axis_size("prow")
    col_procs = lax.axis_size("pcol")
    nz = row_procs // 2
    nbits = col_procs.bit_length() - 1
    cols = ROW_TILES * row_procs // col_procs
    tile_row = tile_pos[:, 0]
    tile_col = tile_pos[:, 1]
    local_row = jnp.clip(tile_row // row_procs, 0, ROW_TILES - 1)
    local_col = jnp.clip(2 * (tile_col // 2 // col_procs) + tile_col % 2, 0, cols - 1)
    listed = tile_row >= 0
    is_upper = listed & (tile_row < 4)
    is_side = listed & (tile_col < 4)
    side_key = local_row * 2 + tile_col % 2
    slot_r = slot_lookup(jnp.where(is_upper, local_col, -1), cols)
    slot_l = slot_lookup(jnp.where(is_side, side_key, -1), 2 * ROW_TILES)
    done = jnp.where(is_upper, local_col, cols + side_key)
    kind = jnp.where(listed, jnp.where(is_upper | is_side, 1, 0), 2)
    done = jnp.where(kind == 1, done, 0)
    place = jnp.stack([local_row, local_col, done, kind]).astype(jnp.int32)

    bf = jnp.bfloat16
    smem = pl.BlockSpec(memory_space=pltpu.SMEM)
    vmem = pl.BlockSpec(memory_space=pltpu.VMEM)
    dma = pltpu.SemaphoreType.DMA
    n = CHUNKS
    rows, side, ext_r, ext_c = pl.pallas_call(
        functools.partial(exchange, nz, nbits, cols),
        out_shape=[
            jax.ShapeDtypeStruct((cols, 4, edge, edge), bf),
            jax.ShapeDtypeStruct((2, ROW_TILES, 2, edge, edge), bf),
            jax.ShapeDtypeStruct((2, 2, edge, edge), bf),
            jax.ShapeDtypeStruct((2, 2, edge, edge), bf),
        ],
        in_specs=[smem, smem, vmem],
        out_specs=[vmem] * 4,
        scratch_shapes=[
            dma((2, n)), dma((2, n)), dma((2, n)), dma((2, n)), dma((2, n)),
            dma((2, nbits, n)), dma((2, n)), dma((5,)), dma((nbits,)), dma((1,)),
        ],
        compiler_params=pltpu.CompilerParams(
            collective_id=0, has_side_effects=True, vmem_limit_bytes=40 * 1024 * 1024),
        name="exchange",
    )(slot_r, slot_l, tiles)
    return pl.pallas_call(
        functools.partial(update, cols),
        out_shape=jax.ShapeDtypeStruct(tiles.shape, bf),
        in_specs=[smem] + [vmem] * 7,
        out_specs=vmem,
        scratch_shapes=[
            pltpu.VMEM((ROW_TILES, edge, 2 * edge), bf),
            pltpu.VMEM((ROW_TILES, edge, 2 * edge), bf),
            pltpu.VMEM((cols, 2 * edge, edge), bf),
            pltpu.VMEM((cols + 2 * ROW_TILES, edge, edge), bf),
        ],
        compiler_params=pltpu.CompilerParams(vmem_limit_bytes=48 * 1024 * 1024),
        name="update",
    )(place, pivots.reshape(2, 2 * edge, 1), inverses, rows, side, ext_r, ext_c, tiles)


def solution(mesh):
    return jax.shard_map(
        local,
        mesh=mesh,
        in_specs=(P(("prow", "pcol"), None, None), P(("prow", "pcol"), None), P(), P()),
        out_specs=P(("prow", "pcol"), None, None),
        check_vma=False,
    )
```

```python
import functools
import jax
import jax.numpy as jnp
from jax import lax
from jax.experimental import pallas as pl
from jax.experimental.pallas import tpu as pltpu
from jax.sharding import PartitionSpec as P

ROW_TILES = 32
CHUNKS = 32
AHEAD = 3
GROUP = 8
MESH = pl.DeviceIdType.MESH


def slot_lookup(keys, count):
    targets = jnp.arange(count, dtype=jnp.int32)
    matches = keys[None, :] == targets[:, None]
    positions = jnp.arange(keys.shape[0], dtype=jnp.int32)
    return jnp.sum(jnp.where(matches, positions[None, :], 0), axis=1)


def exchange(
    nz, nbits, cols,
    slot_r, slot_l, place, order, inverse, tiles,
    out,
    rows, side, ext_r, ext_c, m0, m1, r1, final, mixed, lead,
    up_send, down_send, sib_send, z_recv, sib_recv,
    l_send, l_recv, e_sem, f_send, f_recv,
):
    p = lax.axis_index("prow")
    v = lax.axis_index("pcol")
    z = p // 2
    core = p % 2
    other = p + 1 - 2 * core
    cw = cols // CHUNKS
    rw = ROW_TILES // CHUNKS
    n = CHUNKS
    step = 4
    per = step // cw
    side_lag = 4 * ((2 * nbits + 6) // 4)
    row_lag = 4 * ((2 * nbits + 2 * nz + 1) // 4)
    panels = Panels(cols, order, inverse, rows, side, ext_r, ext_c, tiles, out, m0, m1, r1, final, place)
    panels.lead = lead

    def flip(b):
        return v + b - 2 * b * ((v // b) % 2)

    barrier = pltpu.get_barrier_semaphore()

    @pl.when(z > 0)
    def _():
        pl.semaphore_signal(barrier, inc=1, device_id={"prow": p - 2, "pcol": v}, device_id_type=MESH)

    @pl.when(z < nz - 1)
    def _():
        pl.semaphore_signal(barrier, inc=1, device_id={"prow": p + 2, "pcol": v}, device_id_type=MESH)

    pl.semaphore_signal(barrier, inc=1, device_id={"prow": other, "pcol": v}, device_id_type=MESH)
    for bi in range(nbits):
        pl.semaphore_signal(barrier, inc=1, device_id={"prow": p, "pcol": flip(1 << bi)}, device_id_type=MESH)

    @pl.when(z < 2)
    def _():
        @pl.loop(0, cols)
        def _(c):
            rows[c, p] = tiles[slot_r[c]]

    @pl.when(v < 2)
    def _():
        @pl.loop(0, ROW_TILES)
        def _(i):
            side[v, i, 0] = tiles[slot_l[2 * i]]
            side[v, i, 1] = tiles[slot_l[2 * i + 1]]

    panels.prepare(mixed)
    ends = (z == 0).astype(jnp.int32) + (z == nz - 1).astype(jnp.int32)
    pl.semaphore_wait(barrier, 3 + nbits - ends)

    def block(k, j):
        return rows.at[pl.ds(j * cw, cw), 2 * k + core]

    def up(k, j):
        return pltpu.make_async_remote_copy(
            block(k, j), block(k, j), up_send.at[k, j], z_recv.at[k, j],
            device_id={"prow": p + 2, "pcol": v}, device_id_type=MESH)

    def down(k, j):
        return pltpu.make_async_remote_copy(
            block(k, j), block(k, j), down_send.at[k, j], z_recv.at[k, j],
            device_id={"prow": p - 2, "pcol": v}, device_id_type=MESH)

    def sib(k, j):
        return pltpu.make_async_remote_copy(
            block(k, j), block(k, j), sib_send.at[k, j], sib_recv.at[k, j],
            device_id={"prow": other, "pcol": v}, device_id_type=MESH)

    def sib_in(k, j):
        there = rows.at[pl.ds(j * cw, cw), 2 * k + 1 - core]
        return pltpu.make_async_remote_copy(
            there, there, sib_send.at[k, j], sib_recv.at[k, j],
            device_id={"prow": other, "pcol": v}, device_id_type=MESH)

    def goes_up(k):
        return jnp.logical_and(z >= k, z < nz - 1)

    def goes_down(k):
        return jnp.logical_and(z <= k, z > 0)

    def forward(k, j):
        @pl.when(goes_up(k))
        def _():
            up(k, j).start()

        @pl.when(goes_down(k))
        def _():
            down(k, j).start()

        sib(k, j).start()

    def own(k, j):
        @pl.when(z == k)
        def _():
            forward(k, j)

    def label(s):
        return v if s == 0 else v + 1 - 2 * (v % 2)

    def side_copy(s, j, bi):
        part = side.at[s, pl.ds(j * rw, rw)]
        return pltpu.make_async_remote_copy(
            part, part, l_send.at[s, bi, j], l_recv.at[s, j],
            device_id={"prow": p, "pcol": flip(1 << bi)}, device_id_type=MESH)

    def side_forward(s, j):
        for bi in range(nbits):
            @pl.when(label(s) % (2 << bi) == 0)
            def _():
                side_copy(s, j, bi).start()

    def ext_copy(source, sem, target, recv):
        return pltpu.make_async_remote_copy(
            source, ext_r.at[core], e_sem.at[sem], e_sem.at[recv],
            device_id={"prow": target, "pcol": v}, device_id_type=MESH)

    def ext_forward(source):
        @pl.when(goes_up(1))
        def _():
            ext_copy(source, 0, p + 2, 3).start()

        @pl.when(goes_down(1))
        def _():
            ext_copy(source, 1, p - 2, 3).start()

        ext_copy(source, 2, other, 4).start()

    def corner_copy(source, bi):
        return pltpu.make_async_remote_copy(
            source, ext_c, f_send.at[bi], f_recv.at[0],
            device_id={"prow": p, "pcol": flip(1 << bi)}, device_id_type=MESH)

    def corner_forward(source):
        for bi in range(nbits):
            @pl.when(label(1) % (2 << bi) == 0)
            def _():
                corner_copy(source, bi).start()

    def depth_of(s):
        return sum((label(s) // (1 << bi)) % 2 for bi in range(nbits))

    def compute(j):
        at = j - side_lag

        @pl.when(jnp.logical_and(at >= 0, jnp.logical_and(at < n, at % (step // rw) == 0)))
        def _():
            panels.side_step(at * rw, step)

        @pl.when(j == row_lag)
        def _():
            pltpu.make_async_remote_copy(
                ext_r.at[core], ext_r.at[1 - core], e_sem.at[2], e_sem.at[4],
                device_id={"prow": other, "pcol": v}, device_id_type=MESH).wait_recv()
            panels.set_lead()

        first = j - row_lag

        @pl.when(jnp.logical_and(first >= 0, jnp.logical_and(first < n, first % per == 0)))
        def _():
            for h in range(per):
                sib_in(1, first + h).wait_recv()

                @pl.when(jnp.logical_or(v != 1, (first + h) * cw >= 2))
                def _():
                    sib_in(0, first + h).wait_recv()

            panels.row_step(first * cw, step)

    def side_turn(s, j):
        depth = depth_of(s)
        at = j - 2 * depth + 1

        @pl.when(jnp.logical_and(depth > 0, jnp.logical_and(at >= 0, at < n)))
        def _():
            side_copy(s, at, 0).wait_recv()
            side_forward(s, at)

    for k in range(2):
        for j in range(AHEAD):
            own(k, j)

    @pl.loop(0, n)
    def _(j):
        @pl.when(j + AHEAD < n)
        def _():
            own(0, j + AHEAD)
            own(1, j + AHEAD)

        for s in range(2):
            @pl.when(v == s)
            def _():
                side_forward(s, j)

        for k in (1, 0):
            @pl.when(z != k)
            def _():
                up(k, j).wait_recv()
                forward(k, j)

        for s in range(2):
            side_turn(s, j)

        @pl.when(jnp.logical_and(j == 2 * nbits, z == 1))
        def _():
            ext_forward(side.at[0, 0])
            ext_r[core] = side[0, 0]

        far = jnp.where(z == 0, 1, z - 1)

        @pl.when(jnp.logical_and(j == 2 * nbits + 2 * far, z != 1))
        def _():
            ext_copy(ext_r.at[core], 0, other, 3).wait_recv()
            ext_forward(ext_r.at[core])

        @pl.when(jnp.logical_and(j == 4, v == 1))
        def _():
            for h in range(2 // min(cw, 2)):
                sib_in(0, h).wait_recv()
            corner_forward(rows.at[pl.ds(0, 2), pl.ds(0, 2)])
            ext_c[...] = rows[pl.ds(0, 2), pl.ds(0, 2)]

        @pl.when(jnp.logical_and(j == 4 + 2 * depth_of(1), v != 1))
        def _():
            corner_copy(ext_c, 0).wait_recv()
            corner_forward(ext_c)

        compute(j)

    @pl.loop(n, n + max(side_lag, row_lag))
    def _(j):
        for s in range(2):
            side_turn(s, j)
        compute(j)

    panels.finish_upper()
    panels.finish()

    @pl.loop(0, n)
    def _(j):
        for k in range(2):
            @pl.when(goes_up(k))
            def _():
                up(k, j).wait_send()

            @pl.when(goes_down(k))
            def _():
                down(k, j).wait_send()

            sib(k, j).wait_send()

        for s in range(2):
            for bi in range(nbits):
                @pl.when(label(s) % (2 << bi) == 0)
                def _():
                    side_copy(s, j, bi).wait_send()

    @pl.when(goes_up(1))
    def _():
        ext_copy(ext_r.at[core], 0, other, 3).wait_send()

    @pl.when(goes_down(1))
    def _():
        ext_copy(ext_r.at[core], 1, other, 3).wait_send()

    ext_copy(ext_r.at[core], 2, other, 4).wait_send()
    for bi in range(nbits):
        @pl.when(label(1) % (2 << bi) == 0)
        def _():
            corner_copy(ext_c, bi).wait_send()


def dot(a, b):
    return jnp.dot(a, b, preferred_element_type=jnp.float32)


def pick(order, count):
    spread = lax.broadcasted_iota(jnp.int32, (count, 256), 1)
    return (order == spread).astype(jnp.bfloat16)


class Panels:
    def __init__(self, cols, order, inverse, rows, side, ext_r, ext_c, tiles, out, m0, m1, r1, final, place):
        self.cols, self.order, self.inverse = cols, order, inverse
        self.rows, self.side, self.ext_r, self.ext_c = rows, side, ext_r, ext_c
        self.tiles, self.out, self.place = tiles, out, place
        self.m0, self.m1, self.r1, self.final = m0, m1, r1, final
        self.p = lax.axis_index("prow")
        self.v = lax.axis_index("pcol")

    def prepare(self, mixed):
        for k in range(2):
            mixed[k] = dot(self.inverse[k], pick(self.order[k], 256)).astype(jnp.bfloat16)
        self.mixed = mixed

    def side_step(self, i, step):
        bf = jnp.bfloat16
        ext_c, side, final, cols = self.ext_c, self.side, self.final, self.cols
        corner = jnp.concatenate(
            [jnp.concatenate([ext_c[0, r], ext_c[1, r]], axis=1) for r in range(2)], axis=0)

        def wide(s):
            return jnp.concatenate(
                [side[s, pl.ds(i, step), h].reshape(step * 128, 128) for h in range(2)], axis=1)

        left = wide(0)
        lower = dot(left, self.mixed[0]).astype(bf)
        self.m0[pl.ds(i, step)] = lower.reshape(step, 128, 256)
        right = (wide(1).astype(jnp.float32) - dot(lower, corner)).astype(bf)
        self.m1[pl.ds(i, step)] = dot(right, self.mixed[1]).astype(bf).reshape(step, 128, 256)

        def keep(value):
            for u in range(step):
                for h in range(2):
                    final[cols + 2 * (i + u) + h] = value[u * 128:(u + 1) * 128, h * 128:(h + 1) * 128]

        @pl.when(self.v == 0)
        def _():
            keep(dot(left, self.inverse[0]).astype(bf))

        @pl.when(self.v == 1)
        def _():
            keep(dot(right, self.inverse[1]).astype(bf))

    def pivot_rows(self):
        ext_r = self.ext_r
        return jnp.concatenate(
            [jnp.concatenate([ext_r[r, 0], ext_r[r, 1]], axis=1) for r in range(2)], axis=0)

    def set_lead(self):
        self.lead[...] = dot(self.pivot_rows(), self.mixed[0]).astype(jnp.bfloat16)

    def stacked(self, c, step, half):
        return jnp.concatenate(
            [self.rows[c + u, pl.ds(2 * half, 2)].reshape(256, 128) for u in range(step)], axis=1)

    def row_step(self, c, step):
        top = self.stacked(c, step, 0)
        low = self.stacked(c, step, 1)
        value = (low.astype(jnp.float32) - dot(self.lead[...], top)).astype(jnp.bfloat16)
        for u in range(step):
            self.r1[c + u] = value[:, u * 128:(u + 1) * 128]

    def finish_upper(self):
        bf = jnp.bfloat16
        p, r1, final, cols = self.p, self.r1, self.final, self.cols
        step = 4

        @pl.when(self.v == 0)
        def _():
            value = dot(self.pivot_rows(), self.inverse[0]).astype(bf)
            r1[0] = value[:, :128]
            r1[1] = value[:, 128:]

        @pl.when(p < 2)
        def _():
            part = pick(self.order[0, pl.ds(p * 128, 128)], 128)

            @pl.loop(0, cols, step=step)
            def _(c):
                value = dot(part, self.stacked(c, step, 0)).astype(bf)
                for u in range(step):
                    final[c + u] = value[:, u * 128:(u + 1) * 128]

        @pl.when(jnp.logical_and(p >= 2, p < 4))
        def _():
            part = pick(self.order[1, pl.ds((p - 2) * 128, 128)], 128)

            @pl.loop(0, cols, step=step)
            def _(c):
                low = jnp.concatenate([r1[c + u] for u in range(step)], axis=1)
                value = dot(part, low).astype(bf)
                for u in range(step):
                    final[c + u] = value[:, u * 128:(u + 1) * 128]

    def finish(self):
        place, tiles, rows, final = self.place, self.tiles, self.rows, self.final

        @pl.loop(0, tiles.shape[0], step=GROUP)
        def _(base):
            for u in range(GROUP):
                s = base + u
                i, c, f, kind = place[0, s], place[1, s], place[2, s], place[3, s]
                old = tiles[s].astype(jnp.float32)
                total = dot(self.m0[i], rows[c, pl.ds(0, 2)].reshape(256, 128)) + dot(self.m1[i], self.r1[c])
                other = jnp.where(kind == 1, final[f].astype(jnp.float32), old)
                self.out[s] = jnp.where(kind == 0, old - total, other).astype(jnp.bfloat16)


def local(tiles, tile_pos, pivots, inverses):
    slots, edge, _ = tiles.shape
    row_procs = lax.axis_size("prow")
    col_procs = lax.axis_size("pcol")
    nz = row_procs // 2
    nbits = col_procs.bit_length() - 1
    cols = ROW_TILES * row_procs // col_procs
    tile_row = tile_pos[:, 0]
    tile_col = tile_pos[:, 1]
    local_row = jnp.clip(tile_row // row_procs, 0, ROW_TILES - 1)
    local_col = jnp.clip(2 * (tile_col // 2 // col_procs) + tile_col % 2, 0, cols - 1)
    listed = tile_row >= 0
    is_upper = listed & (tile_row < 4)
    is_side = listed & (tile_col < 4)
    side_key = local_row * 2 + tile_col % 2
    slot_r = slot_lookup(jnp.where(is_upper, local_col, -1), cols)
    slot_l = slot_lookup(jnp.where(is_side, side_key, -1), 2 * ROW_TILES)
    done = jnp.where(is_upper, local_col, cols + side_key)
    kind = jnp.where(listed, jnp.where(is_upper | is_side, 1, 0), 2)
    done = jnp.where(kind == 1, done, 0)
    place = jnp.stack([local_row, local_col, done, kind]).astype(jnp.int32)

    bf = jnp.bfloat16
    smem = pl.BlockSpec(memory_space=pltpu.SMEM)
    vmem = pl.BlockSpec(memory_space=pltpu.VMEM)
    dma = pltpu.SemaphoreType.DMA
    n = CHUNKS
    panel = 2 * edge
    return pl.pallas_call(
        functools.partial(exchange, nz, nbits, cols),
        out_shape=jax.ShapeDtypeStruct(tiles.shape, bf),
        in_specs=[smem, smem, smem, vmem, vmem, vmem],
        out_specs=vmem,
        scratch_shapes=[
            pltpu.VMEM((cols, 4, edge, edge), bf),
            pltpu.VMEM((2, ROW_TILES, 2, edge, edge), bf),
            pltpu.VMEM((2, 2, edge, edge), bf),
            pltpu.VMEM((2, 2, edge, edge), bf),
            pltpu.VMEM((ROW_TILES, edge, panel), bf),
            pltpu.VMEM((ROW_TILES, edge, panel), bf),
            pltpu.VMEM((cols, panel, edge), bf),
            pltpu.VMEM((cols + 2 * ROW_TILES, edge, edge), bf),
            pltpu.VMEM((2, panel, panel), bf),
            pltpu.VMEM((panel, panel), bf),
            dma((2, n)), dma((2, n)), dma((2, n)), dma((2, n)), dma((2, n)),
            dma((2, nbits, n)), dma((2, n)), dma((5,)), dma((nbits,)), dma((1,)),
        ],
        compiler_params=pltpu.CompilerParams(
            collective_id=0, has_side_effects=True, vmem_limit_bytes=48 * 1024 * 1024),
        name="exchange",
    )(slot_r, slot_l, place, pivots.reshape(2, panel, 1), inverses, tiles)


def solution(mesh):
    return jax.shard_map(
        local,
        mesh=mesh,
        in_specs=(P(("prow", "pcol"), None, None), P(("prow", "pcol"), None), P(), P()),
        out_specs=P(("prow", "pcol"), None, None),
        check_vma=False,
    )
```

```python
import functools
import jax
import jax.numpy as jnp
from jax import lax
from jax.experimental import pallas as pl
from jax.experimental.pallas import tpu as pltpu
from jax.sharding import PartitionSpec as P

ROW_TILES = 32
CHUNKS = 32
AHEAD = 3
GROUP = 16
SIDE_CHUNKS = 16
MESH = pl.DeviceIdType.MESH


def slot_lookup(keys, count):
    targets = jnp.arange(count, dtype=jnp.int32)
    matches = keys[None, :] == targets[:, None]
    positions = jnp.arange(keys.shape[0], dtype=jnp.int32)
    return jnp.sum(jnp.where(matches, positions[None, :], 0), axis=1)


def exchange(
    nz, nbits, cols,
    slot_r, slot_l, place, order, inverse, tiles,
    out,
    rows, side, ext_r, ext_c, mix, both, final, mixed, lead,
    up_send, down_send, sib_send, z_recv, sib_recv,
    l_send, l_recv, e_sem, f_send, f_recv,
):
    p = lax.axis_index("prow")
    v = lax.axis_index("pcol")
    z = p // 2
    core = p % 2
    other = p + 1 - 2 * core
    cw = cols // CHUNKS
    ns = SIDE_CHUNKS
    rw = ROW_TILES // ns
    n = CHUNKS
    step = 4
    per = step // cw
    row_lag = 4 * ((3 * nbits + 2 * nz + 1) // 4)
    catch_up = per * (row_lag - 1) // (per - 1)
    panels = Panels(cols, order, inverse, rows, side, ext_r, ext_c, tiles, out, mix, both, final, place)
    panels.lead = lead

    def flip(b):
        return v + b - 2 * b * ((v // b) % 2)

    barrier = pltpu.get_barrier_semaphore()

    @pl.when(z > 0)
    def _():
        pl.semaphore_signal(barrier, inc=1, device_id={"prow": p - 2, "pcol": v}, device_id_type=MESH)

    @pl.when(z < nz - 1)
    def _():
        pl.semaphore_signal(barrier, inc=1, device_id={"prow": p + 2, "pcol": v}, device_id_type=MESH)

    pl.semaphore_signal(barrier, inc=1, device_id={"prow": other, "pcol": v}, device_id_type=MESH)
    for bi in range(nbits):
        pl.semaphore_signal(barrier, inc=1, device_id={"prow": p, "pcol": flip(1 << bi)}, device_id_type=MESH)

    @pl.when(z < 2)
    def _():
        @pl.loop(0, cols)
        def _(c):
            rows[c, p] = tiles[slot_r[c]]

    ends = (z == 0).astype(jnp.int32) + (z == nz - 1).astype(jnp.int32)
    pl.semaphore_wait(barrier, 3 + nbits - ends)

    def block(k, j):
        return rows.at[pl.ds(j * cw, cw), 2 * k + core]

    def up(k, j):
        return pltpu.make_async_remote_copy(
            block(k, j), block(k, j), up_send.at[k, j], z_recv.at[k, j],
            device_id={"prow": p + 2, "pcol": v}, device_id_type=MESH)

    def down(k, j):
        return pltpu.make_async_remote_copy(
            block(k, j), block(k, j), down_send.at[k, j], z_recv.at[k, j],
            device_id={"prow": p - 2, "pcol": v}, device_id_type=MESH)

    def sib(k, j):
        return pltpu.make_async_remote_copy(
            block(k, j), block(k, j), sib_send.at[k, j], sib_recv.at[k, j],
            device_id={"prow": other, "pcol": v}, device_id_type=MESH)

    def sib_in(k, j):
        there = rows.at[pl.ds(j * cw, cw), 2 * k + 1 - core]
        return pltpu.make_async_remote_copy(
            there, there, sib_send.at[k, j], sib_recv.at[k, j],
            device_id={"prow": other, "pcol": v}, device_id_type=MESH)

    def goes_up(k):
        return jnp.logical_and(z >= k, z < nz - 1)

    def goes_down(k):
        return jnp.logical_and(z <= k, z > 0)

    def forward(k, j):
        @pl.when(goes_up(k))
        def _():
            up(k, j).start()

        @pl.when(goes_down(k))
        def _():
            down(k, j).start()

        sib(k, j).start()

    def own(k, j):
        @pl.when(z == k)
        def _():
            forward(k, j)

    def label(s):
        return v if s == 0 else v + 1 - 2 * (v % 2)

    def side_copy(s, j, bi):
        part = side.at[s, pl.ds(j * rw, rw)]
        return pltpu.make_async_remote_copy(
            part, part, l_send.at[s, bi, j], l_recv.at[s, j],
            device_id={"prow": p, "pcol": flip(1 << bi)}, device_id_type=MESH)

    def side_forward(s, j):
        for bi in range(nbits):
            @pl.when(label(s) % (2 << bi) == 0)
            def _():
                side_copy(s, j, bi).start()

    def ext_copy(source, sem, target, recv):
        return pltpu.make_async_remote_copy(
            source, ext_r.at[core], e_sem.at[sem], e_sem.at[recv],
            device_id={"prow": target, "pcol": v}, device_id_type=MESH)

    def ext_forward(source):
        @pl.when(goes_up(1))
        def _():
            ext_copy(source, 0, p + 2, 3).start()

        @pl.when(goes_down(1))
        def _():
            ext_copy(source, 1, p - 2, 3).start()

        ext_copy(source, 2, other, 4).start()

    def corner_copy(source, bi):
        return pltpu.make_async_remote_copy(
            source, ext_c, f_send.at[bi], f_recv.at[0],
            device_id={"prow": p, "pcol": flip(1 << bi)}, device_id_type=MESH)

    def corner_forward(source):
        for bi in range(nbits):
            @pl.when(label(1) % (2 << bi) == 0)
            def _():
                corner_copy(source, bi).start()

    def depth_of(s):
        return sum((label(s) // (1 << bi)) % 2 for bi in range(nbits))

    def side_turns(j):
        @pl.when(j % 4 != 3)
        def _():
            for s in range(2):
                side_turn(s, 3 * (j // 4) + j % 4)

    def compute(j):
        at = 3 * (j // 4) + j % 4 - 2 * nbits - 2

        @pl.when(jnp.logical_and(j % 4 != 3, jnp.logical_and(at >= 0, at < ns)))
        def _():
            @pl.when(at % (step // rw) == 0)
            def _():
                panels.side_step(at * rw, step)

        @pl.when(j == row_lag)
        def _():
            pltpu.make_async_remote_copy(
                ext_r.at[core], ext_r.at[1 - core], e_sem.at[2], e_sem.at[4],
                device_id={"prow": other, "pcol": v}, device_id_type=MESH).wait_recv()
            panels.set_lead()

        early = jnp.logical_and(j >= row_lag, j <= catch_up)
        late = jnp.logical_and(j > catch_up, j % per == 0)
        first = per * jnp.where(j <= catch_up, j - row_lag, j // per - 1)

        @pl.when(jnp.logical_and(jnp.logical_or(early, late), first < n))
        def _():
            for h in range(per):
                sib_in(1, first + h).wait_recv()

                @pl.when(jnp.logical_or(v != 1, (first + h) * cw >= 2))
                def _():
                    sib_in(0, first + h).wait_recv()

            panels.row_step(first * cw, step)

    def side_turn(s, j):
        depth = depth_of(s)
        at = j - 2 * depth + jnp.where(depth > 0, 1, 0)

        @pl.when(jnp.logical_and(at >= 0, at < ns))
        def _():
            @pl.when(depth > 0)
            def _():
                side_copy(s, at, 0).wait_recv()

            side_forward(s, at)

    for k in range(2):
        for j in range(AHEAD):
            own(k, j)

    @pl.when(v < 2)
    def _():
        @pl.loop(0, ROW_TILES)
        def _(i):
            side[v, i, 0] = tiles[slot_l[2 * i]]
            side[v, i, 1] = tiles[slot_l[2 * i + 1]]

    panels.prepare(mixed)

    @pl.loop(0, n)
    def _(j):
        @pl.when(j + AHEAD < n)
        def _():
            own(0, j + AHEAD)
            own(1, j + AHEAD)

        for k in (1, 0):
            @pl.when(z != k)
            def _():
                up(k, j).wait_recv()
                forward(k, j)

        side_turns(j)

        @pl.when(jnp.logical_and(j == 3 * nbits, z == 1))
        def _():
            ext_forward(side.at[0, 0])
            ext_r[core] = side[0, 0]

        far = jnp.where(z == 0, 1, z - 1)

        @pl.when(jnp.logical_and(j == 3 * nbits + 2 * far, z != 1))
        def _():
            ext_copy(ext_r.at[core], 0, other, 3).wait_recv()
            ext_forward(ext_r.at[core])

        @pl.when(jnp.logical_and(j == 4, v == 1))
        def _():
            for h in range(2 // min(cw, 2)):
                sib_in(0, h).wait_recv()
            corner_forward(rows.at[pl.ds(0, 2), pl.ds(0, 2)])
            ext_c[...] = rows[pl.ds(0, 2), pl.ds(0, 2)]

        @pl.when(jnp.logical_and(j == 4 + 2 * depth_of(1), v != 1))
        def _():
            corner_copy(ext_c, 0).wait_recv()
            corner_forward(ext_c)

        compute(j)

    @pl.loop(n, n + 8)
    def _(j):
        side_turns(j)
        compute(j)

    panels.finish_upper()
    panels.finish()

    @pl.loop(0, n)
    def _(j):
        for k in range(2):
            @pl.when(goes_up(k))
            def _():
                up(k, j).wait_send()

            @pl.when(goes_down(k))
            def _():
                down(k, j).wait_send()

            sib(k, j).wait_send()

    @pl.loop(0, ns)
    def _(j):
        for s in range(2):
            for bi in range(nbits):
                @pl.when(label(s) % (2 << bi) == 0)
                def _():
                    side_copy(s, j, bi).wait_send()

    @pl.when(goes_up(1))
    def _():
        ext_copy(ext_r.at[core], 0, other, 3).wait_send()

    @pl.when(goes_down(1))
    def _():
        ext_copy(ext_r.at[core], 1, other, 3).wait_send()

    ext_copy(ext_r.at[core], 2, other, 4).wait_send()
    for bi in range(nbits):
        @pl.when(label(1) % (2 << bi) == 0)
        def _():
            corner_copy(ext_c, bi).wait_send()


def dot(a, b):
    return jnp.dot(a, b, preferred_element_type=jnp.float32)


def pick(order, count):
    spread = lax.broadcasted_iota(jnp.int32, (count, 256), 1)
    return (order == spread).astype(jnp.bfloat16)


class Panels:
    def __init__(self, cols, order, inverse, rows, side, ext_r, ext_c, tiles, out, mix, both, final, place):
        self.cols, self.order, self.inverse = cols, order, inverse
        self.rows, self.side, self.ext_r, self.ext_c = rows, side, ext_r, ext_c
        self.tiles, self.out, self.place = tiles, out, place
        self.mix, self.both, self.final = mix, both, final
        self.p = lax.axis_index("prow")
        self.v = lax.axis_index("pcol")

    def prepare(self, mixed):
        for k in range(2):
            mixed[k] = dot(self.inverse[k], pick(self.order[k], 256)).astype(jnp.bfloat16)
        self.mixed = mixed

    def side_step(self, i, step):
        bf = jnp.bfloat16
        ext_c, side, final, cols = self.ext_c, self.side, self.final, self.cols
        corner = jnp.concatenate(
            [jnp.concatenate([ext_c[0, r], ext_c[1, r]], axis=1) for r in range(2)], axis=0)

        def wide(s):
            return jnp.concatenate(
                [side[s, pl.ds(i, step), h].reshape(step * 128, 128) for h in range(2)], axis=1)

        left = wide(0)
        lower = dot(left, self.mixed[0]).astype(bf)
        self.mix[pl.ds(i, step), :, pl.ds(0, 256)] = lower.reshape(step, 128, 256)
        right = (wide(1).astype(jnp.float32) - dot(lower, corner)).astype(bf)
        self.mix[pl.ds(i, step), :, pl.ds(256, 256)] = dot(right, self.mixed[1]).astype(bf).reshape(step, 128, 256)

        def keep(value):
            for u in range(step):
                for h in range(2):
                    final[cols + 2 * (i + u) + h] = value[u * 128:(u + 1) * 128, h * 128:(h + 1) * 128]

        @pl.when(self.v == 0)
        def _():
            keep(dot(left, self.inverse[0]).astype(bf))

        @pl.when(self.v == 1)
        def _():
            keep(dot(right, self.inverse[1]).astype(bf))

    def pivot_rows(self):
        ext_r = self.ext_r
        return jnp.concatenate(
            [jnp.concatenate([ext_r[r, 0], ext_r[r, 1]], axis=1) for r in range(2)], axis=0)

    def set_lead(self):
        self.lead[...] = dot(self.pivot_rows(), self.mixed[0]).astype(jnp.bfloat16)

    def stacked(self, c, step, half):
        return jnp.concatenate(
            [self.rows[c + u, pl.ds(2 * half, 2)].reshape(256, 128) for u in range(step)], axis=1)

    def row_step(self, c, step):
        top = self.stacked(c, step, 0)
        low = self.stacked(c, step, 1)
        value = (low.astype(jnp.float32) - dot(self.lead[...], top)).astype(jnp.bfloat16)
        for u in range(step):
            self.both[c + u, pl.ds(0, 256)] = top[:, u * 128:(u + 1) * 128]
            self.both[c + u, pl.ds(256, 256)] = value[:, u * 128:(u + 1) * 128]

    def finish_upper(self):
        bf = jnp.bfloat16
        p, both, final, cols = self.p, self.both, self.final, self.cols
        step = 4

        @pl.when(self.v == 0)
        def _():
            value = dot(self.pivot_rows(), self.inverse[0]).astype(bf)
            both[0, pl.ds(256, 256)] = value[:, :128]
            both[1, pl.ds(256, 256)] = value[:, 128:]

        @pl.when(p < 2)
        def _():
            part = pick(self.order[0, pl.ds(p * 128, 128)], 128)

            @pl.loop(0, cols, step=step)
            def _(c):
                value = dot(part, self.stacked(c, step, 0)).astype(bf)
                for u in range(step):
                    final[c + u] = value[:, u * 128:(u + 1) * 128]

        @pl.when(jnp.logical_and(p >= 2, p < 4))
        def _():
            part = pick(self.order[1, pl.ds((p - 2) * 128, 128)], 128)

            @pl.loop(0, cols, step=step)
            def _(c):
                low = jnp.concatenate([both[c + u, pl.ds(256, 256)] for u in range(step)], axis=1)
                value = dot(part, low).astype(bf)
                for u in range(step):
                    final[c + u] = value[:, u * 128:(u + 1) * 128]

    def finish(self):
        place, tiles, final = self.place, self.tiles, self.final

        @pl.loop(0, tiles.shape[0], step=GROUP)
        def _(base):
            for u in range(GROUP):
                s = base + u
                i, c, f, kind = place[0, s], place[1, s], place[2, s], place[3, s]
                base_value = jnp.where(kind == 1, final[f], tiles[s]).astype(jnp.float32)
                total = dot(self.mix[i], self.both[c])
                self.out[s] = (base_value - jnp.where(kind == 0, 1.0, 0.0) * total).astype(jnp.bfloat16)


def local(tiles, tile_pos, pivots, inverses):
    slots, edge, _ = tiles.shape
    row_procs = lax.axis_size("prow")
    col_procs = lax.axis_size("pcol")
    nz = row_procs // 2
    nbits = col_procs.bit_length() - 1
    cols = ROW_TILES * row_procs // col_procs
    tile_row = tile_pos[:, 0]
    tile_col = tile_pos[:, 1]
    local_row = jnp.clip(tile_row // row_procs, 0, ROW_TILES - 1)
    local_col = jnp.clip(2 * (tile_col // 2 // col_procs) + tile_col % 2, 0, cols - 1)
    listed = tile_row >= 0
    is_upper = listed & (tile_row < 4)
    is_side = listed & (tile_col < 4)
    side_key = local_row * 2 + tile_col % 2
    slot_r = slot_lookup(jnp.where(is_upper, local_col, -1), cols)
    slot_l = slot_lookup(jnp.where(is_side, side_key, -1), 2 * ROW_TILES)
    done = jnp.where(is_upper, local_col, cols + side_key)
    kind = jnp.where(listed, jnp.where(is_upper | is_side, 1, 0), 2)
    done = jnp.where(kind == 1, done, 0)
    place = jnp.stack([local_row, local_col, done, kind]).astype(jnp.int32)

    bf = jnp.bfloat16
    smem = pl.BlockSpec(memory_space=pltpu.SMEM)
    vmem = pl.BlockSpec(memory_space=pltpu.VMEM)
    dma = pltpu.SemaphoreType.DMA
    n = CHUNKS
    panel = 2 * edge
    return pl.pallas_call(
        functools.partial(exchange, nz, nbits, cols),
        out_shape=jax.ShapeDtypeStruct(tiles.shape, bf),
        in_specs=[smem, smem, smem, vmem, vmem, vmem],
        out_specs=vmem,
        scratch_shapes=[
            pltpu.VMEM((cols, 4, edge, edge), bf),
            pltpu.VMEM((2, ROW_TILES, 2, edge, edge), bf),
            pltpu.VMEM((2, 2, edge, edge), bf),
            pltpu.VMEM((2, 2, edge, edge), bf),
            pltpu.VMEM((ROW_TILES, edge, 2 * panel), bf),
            pltpu.VMEM((cols, 2 * panel, edge), bf),
            pltpu.VMEM((cols + 2 * ROW_TILES, edge, edge), bf),
            pltpu.VMEM((2, panel, panel), bf),
            pltpu.VMEM((panel, panel), bf),
            dma((2, n)), dma((2, n)), dma((2, n)), dma((2, n)), dma((2, n)),
            dma((2, nbits, SIDE_CHUNKS)), dma((2, SIDE_CHUNKS)), dma((5,)), dma((nbits,)), dma((1,)),
        ],
        compiler_params=pltpu.CompilerParams(
            collective_id=0, has_side_effects=True, vmem_limit_bytes=48 * 1024 * 1024),
        name="exchange",
    )(slot_r, slot_l, place, pivots.reshape(2, panel, 1), inverses, tiles)


def solution(mesh):
    return jax.shard_map(
        local,
        mesh=mesh,
        in_specs=(P(("prow", "pcol"), None, None), P(("prow", "pcol"), None), P(), P()),
        out_specs=P(("prow", "pcol"), None, None),
        check_vma=False,
    )
```

```python
import functools
import jax
import jax.numpy as jnp
from jax import lax
from jax.experimental import pallas as pl
from jax.experimental.pallas import tpu as pltpu
from jax.sharding import PartitionSpec as P

ROW_TILES = 32
AHEAD = 3
GROUP = 16
SIDE_CHUNKS = 16
MESH = pl.DeviceIdType.MESH


def exchange(
    nz, nbits, cols,
    slots, place, order, inverse_in, tiles_in,
    out,
    tiles, inverse, perm, rows, side, ext_r, ext_c, mix, both, final, mixed, lead,
    up_send, down_send, sib_send, z_recv, sib_recv,
    l_send, l_recv, e_sem, f_send, f_recv, in_sem,
):
    p = lax.axis_index("prow")
    v = lax.axis_index("pcol")
    z = p // 2
    core = p % 2
    other = p + 1 - 2 * core
    n = cols
    cw = 1
    stretch = max(n // 32, 1)
    ns = SIDE_CHUNKS
    rw = ROW_TILES // ns
    step = 4
    per = step // cw
    row_lag = 4 * stretch * ((3 * nbits + 2 * nz + 1) // 4)
    catch_up = per * (row_lag - 1) // (per - 1)
    panels = Panels(cols, order, inverse, rows, side, ext_r, ext_c, tiles, out, mix, both, final, place)
    panels.lead = lead

    def flip(b):
        return v + b - 2 * b * ((v // b) % 2)

    load_tiles = pltpu.make_async_copy(tiles_in, tiles, in_sem.at[0])
    load_inverse = pltpu.make_async_copy(inverse_in, inverse, in_sem.at[1])
    load_tiles.start()
    load_inverse.start()
    barrier = pltpu.get_barrier_semaphore()

    @pl.when(z > 0)
    def _():
        pl.semaphore_signal(barrier, inc=1, device_id={"prow": p - 2, "pcol": v}, device_id_type=MESH)

    @pl.when(z < nz - 1)
    def _():
        pl.semaphore_signal(barrier, inc=1, device_id={"prow": p + 2, "pcol": v}, device_id_type=MESH)

    pl.semaphore_signal(barrier, inc=1, device_id={"prow": other, "pcol": v}, device_id_type=MESH)
    for bi in range(nbits):
        pl.semaphore_signal(barrier, inc=1, device_id={"prow": p, "pcol": flip(1 << bi)}, device_id_type=MESH)

    load_tiles.wait()

    @pl.when(z < 2)
    def _():
        @pl.loop(0, cols)
        def _(c):
            rows[c, p] = tiles[slots[c]]

    ends = (z == 0).astype(jnp.int32) + (z == nz - 1).astype(jnp.int32)
    pl.semaphore_wait(barrier, 3 + nbits - ends)

    def block(k, j):
        return rows.at[pl.ds(j * cw, cw), 2 * k + core]

    def up(k, j):
        return pltpu.make_async_remote_copy(
            block(k, j), block(k, j), up_send.at[k, j], z_recv.at[k, j],
            device_id={"prow": p + 2, "pcol": v}, device_id_type=MESH)

    def down(k, j):
        return pltpu.make_async_remote_copy(
            block(k, j), block(k, j), down_send.at[k, j], z_recv.at[k, j],
            device_id={"prow": p - 2, "pcol": v}, device_id_type=MESH)

    def sib(k, j):
        return pltpu.make_async_remote_copy(
            block(k, j), block(k, j), sib_send.at[k, j], sib_recv.at[k, j],
            device_id={"prow": other, "pcol": v}, device_id_type=MESH)

    def sib_in(k, j):
        there = rows.at[pl.ds(j * cw, cw), 2 * k + 1 - core]
        return pltpu.make_async_remote_copy(
            there, there, sib_send.at[k, j], sib_recv.at[k, j],
            device_id={"prow": other, "pcol": v}, device_id_type=MESH)

    def goes_up(k):
        return jnp.logical_and(z >= k, z < nz - 1)

    def goes_down(k):
        return jnp.logical_and(z <= k, z > 0)

    def forward(k, j):
        @pl.when(goes_up(k))
        def _():
            up(k, j).start()

        @pl.when(goes_down(k))
        def _():
            down(k, j).start()

        sib(k, j).start()

    def own(k, j):
        @pl.when(z == k)
        def _():
            forward(k, j)

    def label(s):
        return v if s == 0 else v + 1 - 2 * (v % 2)

    def side_copy(s, j, bi):
        part = side.at[s, pl.ds(j * rw, rw)]
        return pltpu.make_async_remote_copy(
            part, part, l_send.at[s, bi, j], l_recv.at[s, j],
            device_id={"prow": p, "pcol": flip(1 << bi)}, device_id_type=MESH)

    def side_forward(s, j):
        for bi in range(nbits):
            @pl.when(label(s) % (2 << bi) == 0)
            def _():
                side_copy(s, j, bi).start()

    def ext_copy(source, sem, target, recv):
        return pltpu.make_async_remote_copy(
            source, ext_r.at[core], e_sem.at[sem], e_sem.at[recv],
            device_id={"prow": target, "pcol": v}, device_id_type=MESH)

    def ext_forward(source):
        @pl.when(goes_up(1))
        def _():
            ext_copy(source, 0, p + 2, 3).start()

        @pl.when(goes_down(1))
        def _():
            ext_copy(source, 1, p - 2, 3).start()

        ext_copy(source, 2, other, 4).start()

    def corner_copy(source, bi):
        return pltpu.make_async_remote_copy(
            source, ext_c, f_send.at[bi], f_recv.at[0],
            device_id={"prow": p, "pcol": flip(1 << bi)}, device_id_type=MESH)

    def corner_forward(source):
        for bi in range(nbits):
            @pl.when(label(1) % (2 << bi) == 0)
            def _():
                corner_copy(source, bi).start()

    def depth_of(s):
        return sum((label(s) // (1 << bi)) % 2 for bi in range(nbits))

    def side_turns(j):
        slow = j // stretch

        @pl.when(jnp.logical_and(j % stretch == 0, slow % 4 != 3))
        def _():
            for s in range(2):
                side_turn(s, 3 * (slow // 4) + slow % 4)

    def compute(j):
        slow = j // stretch
        at = 3 * (slow // 4) + slow % 4 - 2 * nbits - 2
        live = jnp.logical_and(j % stretch == stretch - 1, slow % 4 != 3)

        @pl.when(jnp.logical_and(live, jnp.logical_and(at >= 0, at < ns)))
        def _():
            @pl.when(at % (step // rw) == 0)
            def _():
                panels.side_step(at * rw, step)

        @pl.when(j == row_lag)
        def _():
            pltpu.make_async_remote_copy(
                ext_r.at[core], ext_r.at[1 - core], e_sem.at[2], e_sem.at[4],
                device_id={"prow": other, "pcol": v}, device_id_type=MESH).wait_recv()
            panels.set_lead()

        early = jnp.logical_and(j >= row_lag, j <= catch_up)
        late = jnp.logical_and(j > catch_up, j % per == 0)
        first = per * jnp.where(j <= catch_up, j - row_lag, j // per - 1)

        @pl.when(jnp.logical_and(jnp.logical_or(early, late), first < n))
        def _():
            for h in range(per):
                sib_in(1, first + h).wait_recv()

                @pl.when(jnp.logical_or(v != 1, (first + h) * cw >= 2))
                def _():
                    sib_in(0, first + h).wait_recv()

            panels.row_step(first * cw, step)

    def side_turn(s, j):
        depth = depth_of(s)
        at = j - 2 * depth + jnp.where(depth > 0, 1, 0)

        @pl.when(jnp.logical_and(at >= 0, at < ns))
        def _():
            @pl.when(depth > 0)
            def _():
                side_copy(s, at, 0).wait_recv()

            side_forward(s, at)

    for k in range(2):
        for j in range(AHEAD):
            own(k, j)

    @pl.when(v < 2)
    def _():
        @pl.loop(0, ROW_TILES)
        def _(i):
            side[v, i, 0] = tiles[slots[cols + 2 * i]]
            side[v, i, 1] = tiles[slots[cols + 2 * i + 1]]

    load_inverse.wait()
    panels.prepare(mixed, perm)

    @pl.loop(0, n)
    def _(j):
        @pl.when(j + AHEAD < n)
        def _():
            own(0, j + AHEAD)
            own(1, j + AHEAD)

        for k in (1, 0):
            @pl.when(z != k)
            def _():
                up(k, j).wait_recv()
                forward(k, j)

        side_turns(j)

        @pl.when(jnp.logical_and(j == stretch * 3 * nbits, z == 1))
        def _():
            ext_forward(side.at[0, 0])
            ext_r[core] = side[0, 0]

        far = jnp.where(z == 0, 1, z - 1)

        @pl.when(jnp.logical_and(j == stretch * (3 * nbits + 2 * far), z != 1))
        def _():
            ext_copy(ext_r.at[core], 0, other, 3).wait_recv()
            ext_forward(ext_r.at[core])

        @pl.when(jnp.logical_and(j == stretch * 4, v == 1))
        def _():
            for h in range(2 // min(cw, 2)):
                sib_in(0, h).wait_recv()
            corner_forward(rows.at[pl.ds(0, 2), pl.ds(0, 2)])
            ext_c[...] = rows[pl.ds(0, 2), pl.ds(0, 2)]

        @pl.when(jnp.logical_and(j == stretch * (4 + 2 * depth_of(1)), v != 1))
        def _():
            corner_copy(ext_c, 0).wait_recv()
            corner_forward(ext_c)

        compute(j)

    @pl.loop(n, n + 8 * stretch)
    def _(j):
        side_turns(j)
        compute(j)

    panels.finish_upper()
    panels.finish()

    @pl.loop(0, n)
    def _(j):
        for k in range(2):
            @pl.when(goes_up(k))
            def _():
                up(k, j).wait_send()

            @pl.when(goes_down(k))
            def _():
                down(k, j).wait_send()

            sib(k, j).wait_send()

    @pl.loop(0, ns)
    def _(j):
        for s in range(2):
            for bi in range(nbits):
                @pl.when(label(s) % (2 << bi) == 0)
                def _():
                    side_copy(s, j, bi).wait_send()

    @pl.when(goes_up(1))
    def _():
        ext_copy(ext_r.at[core], 0, other, 3).wait_send()

    @pl.when(goes_down(1))
    def _():
        ext_copy(ext_r.at[core], 1, other, 3).wait_send()

    ext_copy(ext_r.at[core], 2, other, 4).wait_send()
    for bi in range(nbits):
        @pl.when(label(1) % (2 << bi) == 0)
        def _():
            corner_copy(ext_c, bi).wait_send()


def dot(a, b):
    return jnp.dot(a, b, preferred_element_type=jnp.float32)


class Panels:
    def __init__(self, cols, order, inverse, rows, side, ext_r, ext_c, tiles, out, mix, both, final, place):
        self.cols, self.order, self.inverse = cols, order, inverse
        self.rows, self.side, self.ext_r, self.ext_c = rows, side, ext_r, ext_c
        self.tiles, self.out, self.place = tiles, out, place
        self.mix, self.both, self.final = mix, both, final
        self.p = lax.axis_index("prow")
        self.v = lax.axis_index("pcol")

    def prepare(self, mixed, perm):
        spread = lax.broadcasted_iota(jnp.int32, (256, 256), 0)
        for k in range(2):
            turned = jnp.where(self.order[pl.ds(k, 1), :] == spread, 1.0, 0.0)
            perm[k] = turned.T.astype(jnp.bfloat16)
            mixed[k] = dot(self.inverse[k], perm[k]).astype(jnp.bfloat16)
        self.mixed = mixed
        self.perm = perm

    def side_step(self, i, step):
        bf = jnp.bfloat16
        ext_c, side, final, cols = self.ext_c, self.side, self.final, self.cols
        corner = jnp.concatenate(
            [jnp.concatenate([ext_c[0, r], ext_c[1, r]], axis=1) for r in range(2)], axis=0)

        def wide(s):
            return jnp.concatenate(
                [side[s, pl.ds(i, step), h].reshape(step * 128, 128) for h in range(2)], axis=1)

        left = wide(0)
        lower = dot(left, self.mixed[0]).astype(bf)
        self.mix[pl.ds(i, step), :, pl.ds(0, 256)] = lower.reshape(step, 128, 256)
        right = (wide(1).astype(jnp.float32) - dot(lower, corner)).astype(bf)
        self.mix[pl.ds(i, step), :, pl.ds(256, 256)] = dot(right, self.mixed[1]).astype(bf).reshape(step, 128, 256)

        def keep(value):
            for u in range(step):
                for h in range(2):
                    final[cols + 2 * (i + u) + h] = value[u * 128:(u + 1) * 128, h * 128:(h + 1) * 128]

        @pl.when(self.v == 0)
        def _():
            keep(dot(left, self.inverse[0]).astype(bf))

        @pl.when(self.v == 1)
        def _():
            keep(dot(right, self.inverse[1]).astype(bf))

    def pivot_rows(self):
        ext_r = self.ext_r
        return jnp.concatenate(
            [jnp.concatenate([ext_r[r, 0], ext_r[r, 1]], axis=1) for r in range(2)], axis=0)

    def set_lead(self):
        self.lead[...] = dot(self.pivot_rows(), self.mixed[0]).astype(jnp.bfloat16)

    def stacked(self, c, step, half):
        return jnp.concatenate(
            [self.rows[c + u, pl.ds(2 * half, 2)].reshape(256, 128) for u in range(step)], axis=1)

    def row_step(self, c, step):
        top = self.stacked(c, step, 0)
        low = self.stacked(c, step, 1)
        value = (low.astype(jnp.float32) - dot(self.lead[...], top)).astype(jnp.bfloat16)
        for u in range(step):
            self.both[c + u, pl.ds(0, 256)] = top[:, u * 128:(u + 1) * 128]
            self.both[c + u, pl.ds(256, 256)] = value[:, u * 128:(u + 1) * 128]

    def finish_upper(self):
        bf = jnp.bfloat16
        p, both, final, cols = self.p, self.both, self.final, self.cols
        step = 4

        @pl.when(self.v == 0)
        def _():
            value = dot(self.pivot_rows(), self.inverse[0]).astype(bf)
            both[0, pl.ds(256, 256)] = value[:, :128]
            both[1, pl.ds(256, 256)] = value[:, 128:]

        @pl.when(p < 2)
        def _():
            part = self.perm[0, pl.ds(p * 128, 128)]

            @pl.loop(0, cols, step=step)
            def _(c):
                value = dot(part, self.stacked(c, step, 0)).astype(bf)
                for u in range(step):
                    final[c + u] = value[:, u * 128:(u + 1) * 128]

        @pl.when(jnp.logical_and(p >= 2, p < 4))
        def _():
            part = self.perm[1, pl.ds((p - 2) * 128, 128)]

            @pl.loop(0, cols, step=step)
            def _(c):
                low = jnp.concatenate([both[c + u, pl.ds(256, 256)] for u in range(step)], axis=1)
                value = dot(part, low).astype(bf)
                for u in range(step):
                    final[c + u] = value[:, u * 128:(u + 1) * 128]

    def finish(self):
        place, tiles, final = self.place, self.tiles, self.final

        @pl.loop(0, tiles.shape[0], step=GROUP)
        def _(base):
            for u in range(GROUP):
                s = base + u
                i, c, f, kind = place[0, s], place[1, s], place[2, s], place[3, s]
                base_value = jnp.where(kind == 1, final[f], tiles[s]).astype(jnp.float32)
                total = dot(self.mix[i], self.both[c])
                self.out[s] = (base_value - jnp.where(kind == 0, 1.0, 0.0) * total).astype(jnp.bfloat16)


def local(tiles, tile_pos, pivots, inverses):
    slots, edge, _ = tiles.shape
    row_procs = lax.axis_size("prow")
    col_procs = lax.axis_size("pcol")
    nz = row_procs // 2
    nbits = col_procs.bit_length() - 1
    cols = ROW_TILES * row_procs // col_procs
    tile_row = tile_pos[:, 0]
    tile_col = tile_pos[:, 1]
    local_row = jnp.clip(tile_row // row_procs, 0, ROW_TILES - 1)
    local_col = jnp.clip(2 * (tile_col // 2 // col_procs) + tile_col % 2, 0, cols - 1)
    listed = tile_row >= 0
    is_upper = listed & (tile_row < 4)
    is_side = listed & (tile_col < 4)
    side_key = local_row * 2 + tile_col % 2
    targets = jnp.arange(cols + 2 * ROW_TILES, dtype=jnp.int32)[:, None]
    upper_key = jnp.where(is_upper, local_col, -1)[None, :]
    lower_key = jnp.where(is_side, cols + side_key, -1)[None, :]
    match = jnp.where(targets < cols, upper_key, lower_key) == targets
    found = jnp.sum(jnp.where(match, jnp.arange(slots, dtype=jnp.int32)[None, :], 0), axis=1)
    done = jnp.where(is_upper, local_col, cols + side_key)
    kind = jnp.where(listed, jnp.where(is_upper | is_side, 1, 0), 2)
    done = jnp.where(kind == 1, done, 0)
    place = jnp.stack([local_row, local_col, done, kind]).astype(jnp.int32)

    bf = jnp.bfloat16
    smem = pl.BlockSpec(memory_space=pltpu.SMEM)
    vmem = pl.BlockSpec(memory_space=pltpu.VMEM)
    dma = pltpu.SemaphoreType.DMA
    n = cols
    panel = 2 * edge
    return pl.pallas_call(
        functools.partial(exchange, nz, nbits, cols),
        out_shape=jax.ShapeDtypeStruct(tiles.shape, bf),
        in_specs=[smem, smem, vmem, pl.BlockSpec(memory_space=pl.ANY), pl.BlockSpec(memory_space=pl.ANY)],
        out_specs=vmem,
        scratch_shapes=[
            pltpu.VMEM(tiles.shape, bf),
            pltpu.VMEM((2, panel, panel), bf),
            pltpu.VMEM((2, panel, panel), bf),
            pltpu.VMEM((cols, 4, edge, edge), bf),
            pltpu.VMEM((2, ROW_TILES, 2, edge, edge), bf),
            pltpu.VMEM((2, 2, edge, edge), bf),
            pltpu.VMEM((2, 2, edge, edge), bf),
            pltpu.VMEM((ROW_TILES, edge, 2 * panel), bf),
            pltpu.VMEM((cols, 2 * panel, edge), bf),
            pltpu.VMEM((cols + 2 * ROW_TILES, edge, edge), bf),
            pltpu.VMEM((2, panel, panel), bf),
            pltpu.VMEM((panel, panel), bf),
            dma((2, n)), dma((2, n)), dma((2, n)), dma((2, n)), dma((2, n)),
            dma((2, nbits, SIDE_CHUNKS)), dma((2, SIDE_CHUNKS)), dma((5,)), dma((nbits,)), dma((1,)), dma((2,)),
        ],
        compiler_params=pltpu.CompilerParams(
            collective_id=0, has_side_effects=True, vmem_limit_bytes=48 * 1024 * 1024),
        name="exchange",
    )(found, place, pivots, inverses, tiles)


def solution(mesh):
    return jax.shard_map(
        local,
        mesh=mesh,
        in_specs=(P(("prow", "pcol"), None, None), P(("prow", "pcol"), None), P(), P()),
        out_specs=P(("prow", "pcol"), None, None),
        check_vma=False,
    )
```

```python
import functools
import jax
import jax.numpy as jnp
from jax import lax
from jax.experimental import pallas as pl
from jax.experimental.pallas import tpu as pltpu
from jax.sharding import PartitionSpec as P

ROW_TILES = 32
CHUNKS = 32
AHEAD = (8, 5)
SKEW = 3
WINDOW = 3
GROUP = 16
SIDE_CHUNKS = 16
MESH = pl.DeviceIdType.MESH


def exchange(
    nz, nbits, cols,
    slots, place, order, inverse_in, tiles_in,
    out,
    tiles, inverse, perm, rows, side, ext_r, ext_c, mix, both, final, mixed, lead,
    up_send, down_send, sib_send, z_recv, sib_recv,
    l_send, l_recv, e_sem, f_send, f_recv, in_sem,
):
    p = lax.axis_index("prow")
    v = lax.axis_index("pcol")
    z = p // 2
    core = p % 2
    other = p + 1 - 2 * core
    n = CHUNKS
    cw = cols // n
    stretch = 1
    ns = SIDE_CHUNKS
    rw = ROW_TILES // ns
    step = 4
    per = step // cw
    row_lag = 4 * stretch * ((3 * nbits + 2 * nz + 1) // 4)
    catch_up = per * (row_lag - 1) // (per - 1)
    panels = Panels(cols, order, inverse, rows, side, ext_r, ext_c, tiles, out, mix, both, final, place)
    panels.lead = lead

    def flip(b):
        return v + b - 2 * b * ((v // b) % 2)

    load_tiles = pltpu.make_async_copy(tiles_in, tiles, in_sem.at[0])
    load_inverse = pltpu.make_async_copy(inverse_in, inverse, in_sem.at[1])
    load_tiles.start()
    load_inverse.start()
    barrier = pltpu.get_barrier_semaphore()

    @pl.when(z > 0)
    def _():
        pl.semaphore_signal(barrier, inc=1, device_id={"prow": p - 2, "pcol": v}, device_id_type=MESH)

    @pl.when(z < nz - 1)
    def _():
        pl.semaphore_signal(barrier, inc=1, device_id={"prow": p + 2, "pcol": v}, device_id_type=MESH)

    pl.semaphore_signal(barrier, inc=1, device_id={"prow": other, "pcol": v}, device_id_type=MESH)
    for bi in range(nbits):
        pl.semaphore_signal(barrier, inc=1, device_id={"prow": p, "pcol": flip(1 << bi)}, device_id_type=MESH)

    load_tiles.wait()

    @pl.when(z < 2)
    def _():
        @pl.loop(0, cols)
        def _(c):
            rows[c, p] = tiles[slots[c]]

    ends = (z == 0).astype(jnp.int32) + (z == nz - 1).astype(jnp.int32)
    pl.semaphore_wait(barrier, 3 + nbits - ends)

    def block(k, j):
        return rows.at[pl.ds(j * cw, cw), 2 * k + core]

    def up(k, j):
        return pltpu.make_async_remote_copy(
            block(k, j), block(k, j), up_send.at[k, j], z_recv.at[k, j],
            device_id={"prow": p + 2, "pcol": v}, device_id_type=MESH)

    def down(k, j):
        return pltpu.make_async_remote_copy(
            block(k, j), block(k, j), down_send.at[k, j], z_recv.at[k, j],
            device_id={"prow": p - 2, "pcol": v}, device_id_type=MESH)

    def sib(k, j):
        return pltpu.make_async_remote_copy(
            block(k, j), block(k, j), sib_send.at[k, j], sib_recv.at[k, j],
            device_id={"prow": other, "pcol": v}, device_id_type=MESH)

    def sib_in(k, j):
        there = rows.at[pl.ds(j * cw, cw), 2 * k + 1 - core]
        return pltpu.make_async_remote_copy(
            there, there, sib_send.at[k, j], sib_recv.at[k, j],
            device_id={"prow": other, "pcol": v}, device_id_type=MESH)

    def goes_up(k):
        return jnp.logical_and(z >= k, z < nz - 1)

    def goes_down(k):
        return jnp.logical_and(z <= k, z > 0)

    def forward(k, j):
        @pl.when(goes_up(k))
        def _():
            up(k, j).start()

        @pl.when(goes_down(k))
        def _():
            down(k, j).start()

        sib(k, j).start()

    def own(k, j):
        @pl.when(z == k)
        def _():
            forward(k, j)

    def label(s):
        return v if s == 0 else v + 1 - 2 * (v % 2)

    def side_copy(s, j, bi):
        part = side.at[s, pl.ds(j * rw, rw)]
        return pltpu.make_async_remote_copy(
            part, part, l_send.at[s, bi, j], l_recv.at[s, j],
            device_id={"prow": p, "pcol": flip(1 << bi)}, device_id_type=MESH)

    def side_forward(s, j):
        for bi in range(nbits):
            @pl.when(label(s) % (2 << bi) == 0)
            def _():
                side_copy(s, j, bi).start()

    def ext_copy(source, sem, target, recv):
        return pltpu.make_async_remote_copy(
            source, ext_r.at[core], e_sem.at[sem], e_sem.at[recv],
            device_id={"prow": target, "pcol": v}, device_id_type=MESH)

    def ext_forward(source):
        @pl.when(goes_up(1))
        def _():
            ext_copy(source, 0, p + 2, 3).start()

        @pl.when(goes_down(1))
        def _():
            ext_copy(source, 1, p - 2, 3).start()

        ext_copy(source, 2, other, 4).start()

    def corner_copy(source, bi):
        return pltpu.make_async_remote_copy(
            source, ext_c, f_send.at[bi], f_recv.at[0],
            device_id={"prow": p, "pcol": flip(1 << bi)}, device_id_type=MESH)

    def corner_forward(source):
        for bi in range(nbits):
            @pl.when(label(1) % (2 << bi) == 0)
            def _():
                corner_copy(source, bi).start()

    def depth_of(s):
        return sum((label(s) // (1 << bi)) % 2 for bi in range(nbits))

    def side_turns(j):
        slow = j // stretch

        @pl.when(jnp.logical_and(j % stretch == 0, slow % 4 != 3))
        def _():
            for s in range(2):
                side_turn(s, 3 * (slow // 4) + slow % 4)

    def compute(j):
        slow = j // stretch
        at = 3 * (slow // 4) + slow % 4 - 2 * nbits - 2
        live = jnp.logical_and(j % stretch == stretch - 1, slow % 4 != 3)

        @pl.when(jnp.logical_and(live, jnp.logical_and(at >= 0, at < ns)))
        def _():
            @pl.when(at % (step // rw) == 0)
            def _():
                panels.side_step(at * rw, step)

        @pl.when(j == row_lag)
        def _():
            pltpu.make_async_remote_copy(
                ext_r.at[core], ext_r.at[1 - core], e_sem.at[2], e_sem.at[4],
                device_id={"prow": other, "pcol": v}, device_id_type=MESH).wait_recv()
            panels.set_lead()

        early = jnp.logical_and(j >= row_lag, j <= catch_up)
        late = jnp.logical_and(j > catch_up, j % per == 0)
        first = per * jnp.where(j <= catch_up, j - row_lag, j // per - 1)

        @pl.when(jnp.logical_and(jnp.logical_or(early, late), first < n))
        def _():
            for h in range(per):
                sib_in(1, first + h).wait_recv()

                @pl.when(jnp.logical_or(v != 1, (first + h) * cw >= 2))
                def _():
                    sib_in(0, first + h).wait_recv()

            panels.row_step(first * cw, step)

    def side_turn(s, j):
        depth = depth_of(s)
        at = j - 2 * depth + jnp.where(depth > 0, 1, 0)

        @pl.when(jnp.logical_and(at >= 0, at < ns))
        def _():
            @pl.when(depth > 0)
            def _():
                side_copy(s, at, 0).wait_recv()

            side_forward(s, at)

    for k in range(2):
        for j in range(AHEAD[k]):
            own(k, j)

    @pl.when(v < 2)
    def _():
        @pl.loop(0, ROW_TILES)
        def _(i):
            side[v, i, 0] = tiles[slots[cols + 2 * i]]
            side[v, i, 1] = tiles[slots[cols + 2 * i + 1]]

    load_inverse.wait()
    panels.prepare(mixed, perm)

    def turn(k, j):
        @pl.when(z != k)
        def _():
            up(k, j).wait_recv()
            forward(k, j)

    for j in range(SKEW):
        turn(1, j)

    @pl.loop(0, n)
    def _(j):
        for k in range(2):
            @pl.when(j + AHEAD[k] < n)
            def _():
                own(k, j + AHEAD[k])

        @pl.when(j + SKEW < n)
        def _():
            turn(1, j + SKEW)

        turn(0, j)

        @pl.when(jnp.logical_and(z == 1, jnp.logical_and(goes_up(0), j >= WINDOW)))
        def _():
            up(0, j - WINDOW).wait_send()

        side_turns(j)

        @pl.when(jnp.logical_and(j == stretch * 3 * nbits, z == 1))
        def _():
            ext_forward(side.at[0, 0])
            ext_r[core] = side[0, 0]

        far = jnp.where(z == 0, 1, z - 1)

        @pl.when(jnp.logical_and(j == stretch * (3 * nbits + 2 * far), z != 1))
        def _():
            ext_copy(ext_r.at[core], 0, other, 3).wait_recv()
            ext_forward(ext_r.at[core])

        @pl.when(jnp.logical_and(j == stretch * 4, v == 1))
        def _():
            for h in range(2 // min(cw, 2)):
                sib_in(0, h).wait_recv()
            corner_forward(rows.at[pl.ds(0, 2), pl.ds(0, 2)])
            ext_c[...] = rows[pl.ds(0, 2), pl.ds(0, 2)]

        @pl.when(jnp.logical_and(j == stretch * (4 + 2 * depth_of(1)), v != 1))
        def _():
            corner_copy(ext_c, 0).wait_recv()
            corner_forward(ext_c)

        compute(j)

    @pl.loop(n, n + 8 * stretch)
    def _(j):
        side_turns(j)
        compute(j)

    panels.finish_upper()
    panels.finish()

    @pl.loop(0, n)
    def _(j):
        for k in range(2):
            left = goes_up(k)
            if k == 0:
                left = jnp.logical_and(left, jnp.logical_or(z != 1, j >= n - WINDOW))

            @pl.when(left)
            def _():
                up(k, j).wait_send()

            @pl.when(goes_down(k))
            def _():
                down(k, j).wait_send()

            sib(k, j).wait_send()

    @pl.loop(0, ns)
    def _(j):
        for s in range(2):
            for bi in range(nbits):
                @pl.when(label(s) % (2 << bi) == 0)
                def _():
                    side_copy(s, j, bi).wait_send()

    @pl.when(goes_up(1))
    def _():
        ext_copy(ext_r.at[core], 0, other, 3).wait_send()

    @pl.when(goes_down(1))
    def _():
        ext_copy(ext_r.at[core], 1, other, 3).wait_send()

    ext_copy(ext_r.at[core], 2, other, 4).wait_send()
    for bi in range(nbits):
        @pl.when(label(1) % (2 << bi) == 0)
        def _():
            corner_copy(ext_c, bi).wait_send()


def dot(a, b):
    return jnp.dot(a, b, preferred_element_type=jnp.float32)


class Panels:
    def __init__(self, cols, order, inverse, rows, side, ext_r, ext_c, tiles, out, mix, both, final, place):
        self.cols, self.order, self.inverse = cols, order, inverse
        self.rows, self.side, self.ext_r, self.ext_c = rows, side, ext_r, ext_c
        self.tiles, self.out, self.place = tiles, out, place
        self.mix, self.both, self.final = mix, both, final
        self.p = lax.axis_index("prow")
        self.v = lax.axis_index("pcol")

    def prepare(self, mixed, perm):
        spread = lax.broadcasted_iota(jnp.int32, (256, 256), 0)
        for k in range(2):
            turned = jnp.where(self.order[pl.ds(k, 1), :] == spread, 1.0, 0.0)
            perm[k] = turned.T.astype(jnp.bfloat16)
            mixed[k] = dot(self.inverse[k], perm[k]).astype(jnp.bfloat16)
        self.mixed = mixed
        self.perm = perm

    def side_step(self, i, step):
        bf = jnp.bfloat16
        ext_c, side, final, cols = self.ext_c, self.side, self.final, self.cols
        corner = jnp.concatenate(
            [jnp.concatenate([ext_c[0, r], ext_c[1, r]], axis=1) for r in range(2)], axis=0)

        def wide(s):
            return jnp.concatenate(
                [side[s, pl.ds(i, step), h].reshape(step * 128, 128) for h in range(2)], axis=1)

        left = wide(0)
        lower = dot(left, self.mixed[0]).astype(bf)
        self.mix[pl.ds(i, step), :, pl.ds(0, 256)] = lower.reshape(step, 128, 256)
        right = (wide(1).astype(jnp.float32) - dot(lower, corner)).astype(bf)
        self.mix[pl.ds(i, step), :, pl.ds(256, 256)] = dot(right, self.mixed[1]).astype(bf).reshape(step, 128, 256)

        def keep(value):
            for u in range(step):
                for h in range(2):
                    final[cols + 2 * (i + u) + h] = value[u * 128:(u + 1) * 128, h * 128:(h + 1) * 128]

        @pl.when(self.v == 0)
        def _():
            keep(dot(left, self.inverse[0]).astype(bf))

        @pl.when(self.v == 1)
        def _():
            keep(dot(right, self.inverse[1]).astype(bf))

    def pivot_rows(self):
        ext_r = self.ext_r
        return jnp.concatenate(
            [jnp.concatenate([ext_r[r, 0], ext_r[r, 1]], axis=1) for r in range(2)], axis=0)

    def set_lead(self):
        self.lead[...] = dot(self.pivot_rows(), self.mixed[0]).astype(jnp.bfloat16)

    def stacked(self, c, step, half):
        return jnp.concatenate(
            [self.rows[c + u, pl.ds(2 * half, 2)].reshape(256, 128) for u in range(step)], axis=1)

    def row_step(self, c, step):
        top = self.stacked(c, step, 0)
        low = self.stacked(c, step, 1)
        value = (low.astype(jnp.float32) - dot(self.lead[...], top)).astype(jnp.bfloat16)
        for u in range(step):
            self.both[c + u, pl.ds(0, 256)] = top[:, u * 128:(u + 1) * 128]
            self.both[c + u, pl.ds(256, 256)] = value[:, u * 128:(u + 1) * 128]

    def finish_upper(self):
        bf = jnp.bfloat16
        p, both, final, cols = self.p, self.both, self.final, self.cols
        step = 4

        @pl.when(self.v == 0)
        def _():
            value = dot(self.pivot_rows(), self.inverse[0]).astype(bf)
            both[0, pl.ds(256, 256)] = value[:, :128]
            both[1, pl.ds(256, 256)] = value[:, 128:]

        @pl.when(p < 2)
        def _():
            part = self.perm[0, pl.ds(p * 128, 128)]

            @pl.loop(0, cols, step=step)
            def _(c):
                value = dot(part, self.stacked(c, step, 0)).astype(bf)
                for u in range(step):
                    final[c + u] = value[:, u * 128:(u + 1) * 128]

        @pl.when(jnp.logical_and(p >= 2, p < 4))
        def _():
            part = self.perm[1, pl.ds((p - 2) * 128, 128)]

            @pl.loop(0, cols, step=step)
            def _(c):
                low = jnp.concatenate([both[c + u, pl.ds(256, 256)] for u in range(step)], axis=1)
                value = dot(part, low).astype(bf)
                for u in range(step):
                    final[c + u] = value[:, u * 128:(u + 1) * 128]

    def finish(self):
        place, tiles, final = self.place, self.tiles, self.final

        @pl.loop(0, tiles.shape[0], step=GROUP)
        def _(base):
            for u in range(GROUP):
                s = base + u
                i, c, f, kind = place[0, s], place[1, s], place[2, s], place[3, s]
                base_value = jnp.where(kind == 1, final[f], tiles[s]).astype(jnp.float32)
                total = dot(self.mix[i], self.both[c])
                self.out[s] = (base_value - jnp.where(kind == 0, 1.0, 0.0) * total).astype(jnp.bfloat16)


def local(tiles, tile_pos, pivots, inverses):
    slots, edge, _ = tiles.shape
    row_procs = lax.axis_size("prow")
    col_procs = lax.axis_size("pcol")
    nz = row_procs // 2
    nbits = col_procs.bit_length() - 1
    cols = ROW_TILES * row_procs // col_procs
    tile_row = tile_pos[:, 0]
    tile_col = tile_pos[:, 1]
    local_row = jnp.clip(tile_row // row_procs, 0, ROW_TILES - 1)
    local_col = jnp.clip(2 * (tile_col // 2 // col_procs) + tile_col % 2, 0, cols - 1)
    listed = tile_row >= 0
    is_upper = listed & (tile_row < 4)
    is_side = listed & (tile_col < 4)
    side_key = local_row * 2 + tile_col % 2
    targets = jnp.arange(cols + 2 * ROW_TILES, dtype=jnp.int32)[:, None]
    upper_key = jnp.where(is_upper, local_col, -1)[None, :]
    lower_key = jnp.where(is_side, cols + side_key, -1)[None, :]
    match = jnp.where(targets < cols, upper_key, lower_key) == targets
    found = jnp.sum(jnp.where(match, jnp.arange(slots, dtype=jnp.int32)[None, :], 0), axis=1)
    done = jnp.where(is_upper, local_col, cols + side_key)
    kind = jnp.where(listed, jnp.where(is_upper | is_side, 1, 0), 2)
    done = jnp.where(kind == 1, done, 0)
    place = jnp.stack([local_row, local_col, done, kind]).astype(jnp.int32)

    bf = jnp.bfloat16
    smem = pl.BlockSpec(memory_space=pltpu.SMEM)
    vmem = pl.BlockSpec(memory_space=pltpu.VMEM)
    dma = pltpu.SemaphoreType.DMA
    n = CHUNKS
    panel = 2 * edge
    return pl.pallas_call(
        functools.partial(exchange, nz, nbits, cols),
        out_shape=jax.ShapeDtypeStruct(tiles.shape, bf),
        in_specs=[smem, smem, vmem, pl.BlockSpec(memory_space=pl.ANY), pl.BlockSpec(memory_space=pl.ANY)],
        out_specs=vmem,
        scratch_shapes=[
            pltpu.VMEM(tiles.shape, bf),
            pltpu.VMEM((2, panel, panel), bf),
            pltpu.VMEM((2, panel, panel), bf),
            pltpu.VMEM((cols, 4, edge, edge), bf),
            pltpu.VMEM((2, ROW_TILES, 2, edge, edge), bf),
            pltpu.VMEM((2, 2, edge, edge), bf),
            pltpu.VMEM((2, 2, edge, edge), bf),
            pltpu.VMEM((ROW_TILES, edge, 2 * panel), bf),
            pltpu.VMEM((cols, 2 * panel, edge), bf),
            pltpu.VMEM((cols + 2 * ROW_TILES, edge, edge), bf),
            pltpu.VMEM((2, panel, panel), bf),
            pltpu.VMEM((panel, panel), bf),
            dma((2, n)), dma((2, n)), dma((2, n)), dma((2, n)), dma((2, n)),
            dma((2, nbits, SIDE_CHUNKS)), dma((2, SIDE_CHUNKS)), dma((5,)), dma((nbits,)), dma((1,)), dma((2,)),
        ],
        compiler_params=pltpu.CompilerParams(
            collective_id=0, has_side_effects=True, vmem_limit_bytes=48 * 1024 * 1024),
        name="exchange",
    )(found, place, pivots, inverses, tiles)


def solution(mesh):
    return jax.shard_map(
        local,
        mesh=mesh,
        in_specs=(P(("prow", "pcol"), None, None), P(("prow", "pcol"), None), P(), P()),
        out_specs=P(("prow", "pcol"), None, None),
        check_vma=False,
    )
```

```python
import functools
import jax
import jax.numpy as jnp
from jax import lax
from jax.experimental import pallas as pl
from jax.experimental.pallas import tpu as pltpu
from jax.sharding import PartitionSpec as P

ROW_TILES = 32
CHUNKS = 32
AHEAD = (8, 5)
SKEW = 3
WINDOW = 3
GROUP = 16
SIDE_CHUNKS = 16
MESH = pl.DeviceIdType.MESH


def exchange(
    nz, nbits, cols,
    slots, place, order, inverse_in, tiles_in,
    out,
    tiles, inverse, perm, rows, side, ext_r, ext_c, mix, both, final, mixed, lead,
    up_send, down_send, sib_send, z_recv, sib_recv,
    l_send, l_recv, e_sem, f_send, f_recv, in_sem,
):
    p = lax.axis_index("prow")
    v = lax.axis_index("pcol")
    z = p // 2
    core = p % 2
    other = p + 1 - 2 * core
    n = CHUNKS
    cw = cols // n
    stretch = 1
    ns = SIDE_CHUNKS
    rw = ROW_TILES // ns
    step = 4
    per = step // cw
    row_lag = 4 * stretch * ((3 * nbits + 2 * nz + 1) // 4)
    catch_up = per * (row_lag - 2) // (per - 1)
    panels = Panels(cols, order, inverse, rows, side, ext_r, ext_c, tiles, out, mix, both, final, place)
    panels.lead = lead

    def flip(b):
        return v + b - 2 * b * ((v // b) % 2)

    load_tiles = pltpu.make_async_copy(tiles_in, tiles, in_sem.at[0])
    load_inverse = pltpu.make_async_copy(inverse_in, inverse, in_sem.at[1])
    load_tiles.start()
    load_inverse.start()
    barrier = pltpu.get_barrier_semaphore()

    @pl.when(z > 0)
    def _():
        pl.semaphore_signal(barrier, inc=1, device_id={"prow": p - 2, "pcol": v}, device_id_type=MESH)

    @pl.when(z < nz - 1)
    def _():
        pl.semaphore_signal(barrier, inc=1, device_id={"prow": p + 2, "pcol": v}, device_id_type=MESH)

    pl.semaphore_signal(barrier, inc=1, device_id={"prow": other, "pcol": v}, device_id_type=MESH)
    for bi in range(nbits):
        pl.semaphore_signal(barrier, inc=1, device_id={"prow": p, "pcol": flip(1 << bi)}, device_id_type=MESH)

    load_tiles.wait()

    @pl.when(z < 2)
    def _():
        @pl.loop(0, cols)
        def _(c):
            rows[c, p] = tiles[slots[c]]

    ends = (z == 0).astype(jnp.int32) + (z == nz - 1).astype(jnp.int32)
    pl.semaphore_wait(barrier, 3 + nbits - ends)

    def block(k, j):
        return rows.at[pl.ds(j * cw, cw), 2 * k + core]

    def up(k, j):
        return pltpu.make_async_remote_copy(
            block(k, j), block(k, j), up_send.at[k, j], z_recv.at[k, j],
            device_id={"prow": p + 2, "pcol": v}, device_id_type=MESH)

    def down(k, j):
        return pltpu.make_async_remote_copy(
            block(k, j), block(k, j), down_send.at[k, j], z_recv.at[k, j],
            device_id={"prow": p - 2, "pcol": v}, device_id_type=MESH)

    def sib(k, j):
        return pltpu.make_async_remote_copy(
            block(k, j), block(k, j), sib_send.at[k, j], sib_recv.at[k, j],
            device_id={"prow": other, "pcol": v}, device_id_type=MESH)

    def sib_in(k, j):
        there = rows.at[pl.ds(j * cw, cw), 2 * k + 1 - core]
        return pltpu.make_async_remote_copy(
            there, there, sib_send.at[k, j], sib_recv.at[k, j],
            device_id={"prow": other, "pcol": v}, device_id_type=MESH)

    def goes_up(k):
        return jnp.logical_and(z >= k, z < nz - 1)

    def goes_down(k):
        return jnp.logical_and(z <= k, z > 0)

    def forward(k, j):
        @pl.when(goes_up(k))
        def _():
            up(k, j).start()

        @pl.when(goes_down(k))
        def _():
            down(k, j).start()

        sib(k, j).start()

    def own(k, j):
        @pl.when(z == k)
        def _():
            forward(k, j)

    def label(s):
        return v if s == 0 else v + 1 - 2 * (v % 2)

    def side_copy(s, j, bi):
        part = side.at[s, pl.ds(j * rw, rw)]
        return pltpu.make_async_remote_copy(
            part, part, l_send.at[s, bi, j], l_recv.at[s, j],
            device_id={"prow": p, "pcol": flip(1 << bi)}, device_id_type=MESH)

    def side_forward(s, j):
        for bi in range(nbits):
            @pl.when(label(s) % (2 << bi) == 0)
            def _():
                side_copy(s, j, bi).start()

    def ext_copy(source, sem, target, recv):
        return pltpu.make_async_remote_copy(
            source, ext_r.at[core], e_sem.at[sem], e_sem.at[recv],
            device_id={"prow": target, "pcol": v}, device_id_type=MESH)

    def ext_forward(source):
        @pl.when(goes_up(1))
        def _():
            ext_copy(source, 0, p + 2, 3).start()

        @pl.when(goes_down(1))
        def _():
            ext_copy(source, 1, p - 2, 3).start()

        ext_copy(source, 2, other, 4).start()

    def corner_copy(source, bi):
        return pltpu.make_async_remote_copy(
            source, ext_c, f_send.at[bi], f_recv.at[0],
            device_id={"prow": p, "pcol": flip(1 << bi)}, device_id_type=MESH)

    def corner_forward(source):
        for bi in range(nbits):
            @pl.when(label(1) % (2 << bi) == 0)
            def _():
                corner_copy(source, bi).start()

    def depth_of(s):
        return sum((label(s) // (1 << bi)) % 2 for bi in range(nbits))

    def side_turns(j):
        slow = j // stretch

        @pl.when(jnp.logical_and(j % stretch == 0, slow % 4 != 3))
        def _():
            for s in range(2):
                side_turn(s, 3 * (slow // 4) + slow % 4)

    def compute(j):
        slow = j // stretch
        at = 3 * (slow // 4) + slow % 4 - 2 * nbits - 2
        live = jnp.logical_and(j % stretch == stretch - 1, slow % 4 != 3)

        @pl.when(jnp.logical_and(live, jnp.logical_and(at >= 0, at < ns)))
        def _():
            panels.side_step(at * rw, rw)

        @pl.when(j == row_lag)
        def _():
            pltpu.make_async_remote_copy(
                ext_r.at[core], ext_r.at[1 - core], e_sem.at[2], e_sem.at[4],
                device_id={"prow": other, "pcol": v}, device_id_type=MESH).wait_recv()
            panels.set_lead()

        early = jnp.logical_and(j >= row_lag, j <= catch_up)
        late = jnp.logical_and(j > catch_up, j % per == 0)
        first = per * jnp.where(j <= catch_up, j - row_lag, j // per - 2)

        @pl.when(jnp.logical_and(jnp.logical_or(early, late), first < n))
        def _():
            for h in range(per):
                sib_in(1, first + h).wait_recv()

                @pl.when(jnp.logical_or(v != 1, (first + h) * cw >= 2))
                def _():
                    sib_in(0, first + h).wait_recv()

            panels.row_step(first * cw, step)

    def side_turn(s, j):
        depth = depth_of(s)
        at = j - 2 * depth + jnp.where(depth > 0, 1, 0)

        @pl.when(jnp.logical_and(at >= 0, at < ns))
        def _():
            @pl.when(depth > 0)
            def _():
                side_copy(s, at, 0).wait_recv()

            side_forward(s, at)

    for k in range(2):
        for j in range(AHEAD[k]):
            own(k, j)

    @pl.when(v < 2)
    def _():
        @pl.loop(0, ROW_TILES)
        def _(i):
            side[v, i, 0] = tiles[slots[cols + 2 * i]]
            side[v, i, 1] = tiles[slots[cols + 2 * i + 1]]

    load_inverse.wait()
    panels.prepare(mixed, perm)

    def turn(k, j):
        @pl.when(z != k)
        def _():
            up(k, j).wait_recv()
            forward(k, j)

    for j in range(SKEW):
        turn(1, j)

    @pl.loop(0, n)
    def _(j):
        for k in range(2):
            @pl.when(j + AHEAD[k] < n)
            def _():
                own(k, j + AHEAD[k])

        @pl.when(j + SKEW < n)
        def _():
            turn(1, j + SKEW)

        turn(0, j)

        @pl.when(jnp.logical_and(z == 1, jnp.logical_and(goes_up(0), j >= WINDOW)))
        def _():
            up(0, j - WINDOW).wait_send()

        side_turns(j)

        @pl.when(jnp.logical_and(j == stretch * 3 * nbits, z == 1))
        def _():
            ext_forward(side.at[0, 0])
            ext_r[core] = side[0, 0]

        far = jnp.where(z == 0, 1, z - 1)

        @pl.when(jnp.logical_and(j == stretch * (3 * nbits + 2 * far), z != 1))
        def _():
            ext_copy(ext_r.at[core], 0, other, 3).wait_recv()
            ext_forward(ext_r.at[core])

        @pl.when(jnp.logical_and(j == stretch * 4, v == 1))
        def _():
            for h in range(2 // min(cw, 2)):
                sib_in(0, h).wait_recv()
            corner_forward(rows.at[pl.ds(0, 2), pl.ds(0, 2)])
            ext_c[...] = rows[pl.ds(0, 2), pl.ds(0, 2)]

        @pl.when(jnp.logical_and(j == stretch * (4 + 2 * depth_of(1)), v != 1))
        def _():
            corner_copy(ext_c, 0).wait_recv()
            corner_forward(ext_c)

        compute(j)

    @pl.loop(n, n + 8 * stretch)
    def _(j):
        side_turns(j)
        compute(j)

    panels.finish_upper()
    panels.finish()

    @pl.loop(0, n)
    def _(j):
        for k in range(2):
            left = goes_up(k)
            if k == 0:
                left = jnp.logical_and(left, jnp.logical_or(z != 1, j >= n - WINDOW))

            @pl.when(left)
            def _():
                up(k, j).wait_send()

            @pl.when(goes_down(k))
            def _():
                down(k, j).wait_send()

            sib(k, j).wait_send()

    @pl.loop(0, ns)
    def _(j):
        for s in range(2):
            for bi in range(nbits):
                @pl.when(label(s) % (2 << bi) == 0)
                def _():
                    side_copy(s, j, bi).wait_send()

    @pl.when(goes_up(1))
    def _():
        ext_copy(ext_r.at[core], 0, other, 3).wait_send()

    @pl.when(goes_down(1))
    def _():
        ext_copy(ext_r.at[core], 1, other, 3).wait_send()

    ext_copy(ext_r.at[core], 2, other, 4).wait_send()
    for bi in range(nbits):
        @pl.when(label(1) % (2 << bi) == 0)
        def _():
            corner_copy(ext_c, bi).wait_send()


def dot(a, b):
    return jnp.dot(a, b, preferred_element_type=jnp.float32)


class Panels:
    def __init__(self, cols, order, inverse, rows, side, ext_r, ext_c, tiles, out, mix, both, final, place):
        self.cols, self.order, self.inverse = cols, order, inverse
        self.rows, self.side, self.ext_r, self.ext_c = rows, side, ext_r, ext_c
        self.tiles, self.out, self.place = tiles, out, place
        self.mix, self.both, self.final = mix, both, final
        self.p = lax.axis_index("prow")
        self.v = lax.axis_index("pcol")

    def prepare(self, mixed, perm):
        spread = lax.broadcasted_iota(jnp.int32, (256, 256), 0)
        for k in range(2):
            turned = jnp.where(self.order[pl.ds(k, 1), :] == spread, 1.0, 0.0)
            perm[k] = turned.T.astype(jnp.bfloat16)
            mixed[k] = dot(self.inverse[k], perm[k]).astype(jnp.bfloat16)
        self.mixed = mixed
        self.perm = perm

    def side_step(self, i, step):
        bf = jnp.bfloat16
        ext_c, side, final, cols = self.ext_c, self.side, self.final, self.cols
        corner = jnp.concatenate(
            [jnp.concatenate([ext_c[0, r], ext_c[1, r]], axis=1) for r in range(2)], axis=0)

        def wide(s):
            return jnp.concatenate(
                [side[s, pl.ds(i, step), h].reshape(step * 128, 128) for h in range(2)], axis=1)

        left = wide(0)
        lower = dot(left, self.mixed[0]).astype(bf)
        self.mix[pl.ds(i, step), :, pl.ds(0, 256)] = lower.reshape(step, 128, 256)
        right = (wide(1).astype(jnp.float32) - dot(lower, corner)).astype(bf)
        self.mix[pl.ds(i, step), :, pl.ds(256, 256)] = dot(right, self.mixed[1]).astype(bf).reshape(step, 128, 256)

        def keep(value):
            for u in range(step):
                for h in range(2):
                    final[cols + 2 * (i + u) + h] = value[u * 128:(u + 1) * 128, h * 128:(h + 1) * 128]

        @pl.when(self.v == 0)
        def _():
            keep(dot(left, self.inverse[0]).astype(bf))

        @pl.when(self.v == 1)
        def _():
            keep(dot(right, self.inverse[1]).astype(bf))

    def pivot_rows(self):
        ext_r = self.ext_r
        return jnp.concatenate(
            [jnp.concatenate([ext_r[r, 0], ext_r[r, 1]], axis=1) for r in range(2)], axis=0)

    def set_lead(self):
        self.lead[...] = dot(self.pivot_rows(), self.mixed[0]).astype(jnp.bfloat16)

    def stacked(self, c, step, half):
        return jnp.concatenate(
            [self.rows[c + u, pl.ds(2 * half, 2)].reshape(256, 128) for u in range(step)], axis=1)

    def row_step(self, c, step):
        top = self.stacked(c, step, 0)
        low = self.stacked(c, step, 1)
        value = (low.astype(jnp.float32) - dot(self.lead[...], top)).astype(jnp.bfloat16)
        for u in range(step):
            self.both[c + u, pl.ds(0, 256)] = top[:, u * 128:(u + 1) * 128]
            self.both[c + u, pl.ds(256, 256)] = value[:, u * 128:(u + 1) * 128]

    def finish_upper(self):
        bf = jnp.bfloat16
        p, both, final, cols = self.p, self.both, self.final, self.cols
        step = 4

        @pl.when(self.v == 0)
        def _():
            value = dot(self.pivot_rows(), self.inverse[0]).astype(bf)
            both[0, pl.ds(256, 256)] = value[:, :128]
            both[1, pl.ds(256, 256)] = value[:, 128:]

        @pl.when(p < 2)
        def _():
            part = self.perm[0, pl.ds(p * 128, 128)]

            @pl.loop(0, cols, step=step)
            def _(c):
                value = dot(part, self.stacked(c, step, 0)).astype(bf)
                for u in range(step):
                    final[c + u] = value[:, u * 128:(u + 1) * 128]

        @pl.when(jnp.logical_and(p >= 2, p < 4))
        def _():
            part = self.perm[1, pl.ds((p - 2) * 128, 128)]

            @pl.loop(0, cols, step=step)
            def _(c):
                low = jnp.concatenate([both[c + u, pl.ds(256, 256)] for u in range(step)], axis=1)
                value = dot(part, low).astype(bf)
                for u in range(step):
                    final[c + u] = value[:, u * 128:(u + 1) * 128]

    def finish(self):
        place, tiles, final = self.place, self.tiles, self.final

        @pl.loop(0, tiles.shape[0], step=GROUP)
        def _(base):
            for u in range(GROUP):
                s = base + u
                i, c, f, kind = place[0, s], place[1, s], place[2, s], place[3, s]
                base_value = jnp.where(kind == 1, final[f], tiles[s]).astype(jnp.float32)
                total = dot(self.mix[i], self.both[c])
                self.out[s] = (base_value - jnp.where(kind == 0, 1.0, 0.0) * total).astype(jnp.bfloat16)


def local(tiles, tile_pos, pivots, inverses):
    slots, edge, _ = tiles.shape
    row_procs = lax.axis_size("prow")
    col_procs = lax.axis_size("pcol")
    nz = row_procs // 2
    nbits = col_procs.bit_length() - 1
    cols = ROW_TILES * row_procs // col_procs
    tile_row = tile_pos[:, 0]
    tile_col = tile_pos[:, 1]
    local_row = jnp.clip(tile_row // row_procs, 0, ROW_TILES - 1)
    local_col = jnp.clip(2 * (tile_col // 2 // col_procs) + tile_col % 2, 0, cols - 1)
    listed = tile_row >= 0
    is_upper = listed & (tile_row < 4)
    is_side = listed & (tile_col < 4)
    side_key = local_row * 2 + tile_col % 2
    targets = jnp.arange(cols + 2 * ROW_TILES, dtype=jnp.int32)[:, None]
    upper_key = jnp.where(is_upper, local_col, -1)[None, :]
    lower_key = jnp.where(is_side, cols + side_key, -1)[None, :]
    match = jnp.where(targets < cols, upper_key, lower_key) == targets
    found = jnp.sum(jnp.where(match, jnp.arange(slots, dtype=jnp.int32)[None, :], 0), axis=1)
    done = jnp.where(is_upper, local_col, cols + side_key)
    kind = jnp.where(listed, jnp.where(is_upper | is_side, 1, 0), 2)
    done = jnp.where(kind == 1, done, 0)
    place = jnp.stack([local_row, local_col, done, kind]).astype(jnp.int32)

    bf = jnp.bfloat16
    smem = pl.BlockSpec(memory_space=pltpu.SMEM)
    vmem = pl.BlockSpec(memory_space=pltpu.VMEM)
    dma = pltpu.SemaphoreType.DMA
    n = CHUNKS
    panel = 2 * edge
    return pl.pallas_call(
        functools.partial(exchange, nz, nbits, cols),
        out_shape=jax.ShapeDtypeStruct(tiles.shape, bf),
        in_specs=[smem, smem, vmem, pl.BlockSpec(memory_space=pl.ANY), pl.BlockSpec(memory_space=pl.ANY)],
        out_specs=vmem,
        scratch_shapes=[
            pltpu.VMEM(tiles.shape, bf),
            pltpu.VMEM((2, panel, panel), bf),
            pltpu.VMEM((2, panel, panel), bf),
            pltpu.VMEM((cols, 4, edge, edge), bf),
            pltpu.VMEM((2, ROW_TILES, 2, edge, edge), bf),
            pltpu.VMEM((2, 2, edge, edge), bf),
            pltpu.VMEM((2, 2, edge, edge), bf),
            pltpu.VMEM((ROW_TILES, edge, 2 * panel), bf),
            pltpu.VMEM((cols, 2 * panel, edge), bf),
            pltpu.VMEM((cols + 2 * ROW_TILES, edge, edge), bf),
            pltpu.VMEM((2, panel, panel), bf),
            pltpu.VMEM((panel, panel), bf),
            dma((2, n)), dma((2, n)), dma((2, n)), dma((2, n)), dma((2, n)),
            dma((2, nbits, SIDE_CHUNKS)), dma((2, SIDE_CHUNKS)), dma((5,)), dma((nbits,)), dma((1,)), dma((2,)),
        ],
        compiler_params=pltpu.CompilerParams(
            collective_id=0, has_side_effects=True, vmem_limit_bytes=48 * 1024 * 1024),
        name="exchange",
    )(found, place, pivots, inverses, tiles)


def solution(mesh):
    return jax.shard_map(
        local,
        mesh=mesh,
        in_specs=(P(("prow", "pcol"), None, None), P(("prow", "pcol"), None), P(), P()),
        out_specs=P(("prow", "pcol"), None, None),
        check_vma=False,
    )
```

```python
import functools
import jax
import jax.numpy as jnp
from jax import lax
from jax.experimental import pallas as pl
from jax.experimental.pallas import tpu as pltpu
from jax.sharding import PartitionSpec as P

ROW_TILES = 32
CHUNKS = 32
AHEAD = (8, 5)
SKEW = 3
WINDOW = 3
GROUP = 32
SIDE_CHUNKS = 16
MESH = pl.DeviceIdType.MESH


def exchange(
    nz, nbits, cols,
    slots, place, order, inverse_in, tiles_in,
    out,
    tiles, inverse, perm, rows, side, ext_r, ext_c, mix, both, final, mixed, lead,
    up_send, down_send, sib_send, z_recv, sib_recv,
    l_send, l_recv, e_sem, f_send, f_recv, in_sem,
):
    p = lax.axis_index("prow")
    v = lax.axis_index("pcol")
    z = p // 2
    core = p % 2
    other = p + 1 - 2 * core
    n = CHUNKS
    cw = cols // n
    stretch = 1
    ns = SIDE_CHUNKS
    rw = ROW_TILES // ns
    step = 4
    per = step // cw
    row_lag = 4 * stretch * ((3 * nbits + 2 * nz + 1) // 4)
    catch_up = per * (row_lag - 2) // (per - 1)
    panels = Panels(cols, order, inverse, rows, side, ext_r, ext_c, tiles, out, mix, both, final, place)
    panels.lead = lead

    def flip(b):
        return v + b - 2 * b * ((v // b) % 2)

    load_tiles = pltpu.make_async_copy(tiles_in, tiles, in_sem.at[0])
    load_inverse = pltpu.make_async_copy(inverse_in, inverse, in_sem.at[1])
    load_tiles.start()
    load_inverse.start()
    barrier = pltpu.get_barrier_semaphore()

    @pl.when(z > 0)
    def _():
        pl.semaphore_signal(barrier, inc=1, device_id={"prow": p - 2, "pcol": v}, device_id_type=MESH)

    @pl.when(z < nz - 1)
    def _():
        pl.semaphore_signal(barrier, inc=1, device_id={"prow": p + 2, "pcol": v}, device_id_type=MESH)

    pl.semaphore_signal(barrier, inc=1, device_id={"prow": other, "pcol": v}, device_id_type=MESH)
    for bi in range(nbits):
        pl.semaphore_signal(barrier, inc=1, device_id={"prow": p, "pcol": flip(1 << bi)}, device_id_type=MESH)

    load_tiles.wait()

    @pl.when(z < 2)
    def _():
        @pl.loop(0, cols)
        def _(c):
            rows[c, p] = tiles[slots[c]]

    ends = (z == 0).astype(jnp.int32) + (z == nz - 1).astype(jnp.int32)
    pl.semaphore_wait(barrier, 3 + nbits - ends)

    def block(k, j):
        return rows.at[pl.ds(j * cw, cw), 2 * k + core]

    def up(k, j):
        return pltpu.make_async_remote_copy(
            block(k, j), block(k, j), up_send.at[k, j], z_recv.at[k, j],
            device_id={"prow": p + 2, "pcol": v}, device_id_type=MESH)

    def down(k, j):
        return pltpu.make_async_remote_copy(
            block(k, j), block(k, j), down_send.at[k, j], z_recv.at[k, j],
            device_id={"prow": p - 2, "pcol": v}, device_id_type=MESH)

    def sib(k, j):
        return pltpu.make_async_remote_copy(
            block(k, j), block(k, j), sib_send.at[k, j], sib_recv.at[k, j],
            device_id={"prow": other, "pcol": v}, device_id_type=MESH)

    def sib_in(k, j):
        there = rows.at[pl.ds(j * cw, cw), 2 * k + 1 - core]
        return pltpu.make_async_remote_copy(
            there, there, sib_send.at[k, j], sib_recv.at[k, j],
            device_id={"prow": other, "pcol": v}, device_id_type=MESH)

    def goes_up(k):
        return jnp.logical_and(z >= k, z < nz - 1)

    def goes_down(k):
        return jnp.logical_and(z <= k, z > 0)

    def forward(k, j):
        @pl.when(goes_up(k))
        def _():
            up(k, j).start()

        @pl.when(goes_down(k))
        def _():
            down(k, j).start()

        sib(k, j).start()

    def own(k, j):
        @pl.when(z == k)
        def _():
            forward(k, j)

    def label(s):
        return v if s == 0 else v + 1 - 2 * (v % 2)

    def side_copy(s, j, bi):
        part = side.at[s, pl.ds(j * rw, rw)]
        return pltpu.make_async_remote_copy(
            part, part, l_send.at[s, bi, j], l_recv.at[s, j],
            device_id={"prow": p, "pcol": flip(1 << bi)}, device_id_type=MESH)

    def side_forward(s, j):
        for bi in range(nbits):
            @pl.when(label(s) % (2 << bi) == 0)
            def _():
                side_copy(s, j, bi).start()

    def ext_copy(source, sem, target, recv):
        return pltpu.make_async_remote_copy(
            source, ext_r.at[core], e_sem.at[sem], e_sem.at[recv],
            device_id={"prow": target, "pcol": v}, device_id_type=MESH)

    def ext_forward(source):
        @pl.when(goes_up(1))
        def _():
            ext_copy(source, 0, p + 2, 3).start()

        @pl.when(goes_down(1))
        def _():
            ext_copy(source, 1, p - 2, 3).start()

        ext_copy(source, 2, other, 4).start()

    def corner_copy(source, bi):
        return pltpu.make_async_remote_copy(
            source, ext_c, f_send.at[bi], f_recv.at[0],
            device_id={"prow": p, "pcol": flip(1 << bi)}, device_id_type=MESH)

    def corner_forward(source):
        for bi in range(nbits):
            @pl.when(label(1) % (2 << bi) == 0)
            def _():
                corner_copy(source, bi).start()

    def depth_of(s):
        return sum((label(s) // (1 << bi)) % 2 for bi in range(nbits))

    def side_turns(j):
        slow = j // stretch

        @pl.when(jnp.logical_and(j % stretch == 0, slow % 4 != 3))
        def _():
            for s in range(2):
                side_turn(s, 3 * (slow // 4) + slow % 4)

    def compute(j):
        slow = j // stretch
        at = 3 * (slow // 4) + slow % 4 - 2 * nbits - 2
        live = jnp.logical_and(j % stretch == stretch - 1, slow % 4 != 3)

        @pl.when(jnp.logical_and(live, jnp.logical_and(at >= 0, at < ns)))
        def _():
            panels.side_step(at * rw, rw)

        @pl.when(j == row_lag)
        def _():
            pltpu.make_async_remote_copy(
                ext_r.at[core], ext_r.at[1 - core], e_sem.at[2], e_sem.at[4],
                device_id={"prow": other, "pcol": v}, device_id_type=MESH).wait_recv()
            panels.set_lead()

        early = jnp.logical_and(j >= row_lag, j <= catch_up)
        late = jnp.logical_and(j > catch_up, j % per == 0)
        first = per * jnp.where(j <= catch_up, j - row_lag, j // per - 2)

        @pl.when(jnp.logical_and(jnp.logical_or(early, late), first < n))
        def _():
            for h in range(per):
                sib_in(1, first + h).wait_recv()

                @pl.when(jnp.logical_or(v != 1, (first + h) * cw >= 2))
                def _():
                    sib_in(0, first + h).wait_recv()

            panels.row_step(first * cw, step)

    def side_turn(s, j):
        depth = depth_of(s)
        at = j - 2 * depth + jnp.where(depth > 0, 1, 0)

        @pl.when(jnp.logical_and(at >= 0, at < ns))
        def _():
            @pl.when(depth > 0)
            def _():
                side_copy(s, at, 0).wait_recv()

            side_forward(s, at)

    for k in range(2):
        for j in range(AHEAD[k]):
            own(k, j)

    @pl.when(v < 2)
    def _():
        @pl.loop(0, ROW_TILES)
        def _(i):
            side[v, i, 0] = tiles[slots[cols + 2 * i]]
            side[v, i, 1] = tiles[slots[cols + 2 * i + 1]]

    load_inverse.wait()
    panels.prepare(mixed, perm)

    def turn(k, j):
        @pl.when(z != k)
        def _():
            up(k, j).wait_recv()
            forward(k, j)

    for j in range(SKEW):
        turn(1, j)

    @pl.loop(0, n)
    def _(j):
        for k in range(2):
            @pl.when(j + AHEAD[k] < n)
            def _():
                own(k, j + AHEAD[k])

        @pl.when(j + SKEW < n)
        def _():
            turn(1, j + SKEW)

        turn(0, j)

        @pl.when(jnp.logical_and(z == 1, jnp.logical_and(goes_up(0), j >= WINDOW)))
        def _():
            up(0, j - WINDOW).wait_send()

        side_turns(j)

        @pl.when(jnp.logical_and(j == stretch * 3 * nbits, z == 1))
        def _():
            ext_forward(side.at[0, 0])
            ext_r[core] = side[0, 0]

        far = jnp.where(z == 0, 1, z - 1)

        @pl.when(jnp.logical_and(j == stretch * (3 * nbits + 2 * far), z != 1))
        def _():
            ext_copy(ext_r.at[core], 0, other, 3).wait_recv()
            ext_forward(ext_r.at[core])

        @pl.when(jnp.logical_and(j == stretch * 4, v == 1))
        def _():
            for h in range(2 // min(cw, 2)):
                sib_in(0, h).wait_recv()
            corner_forward(rows.at[pl.ds(0, 2), pl.ds(0, 2)])
            ext_c[...] = rows[pl.ds(0, 2), pl.ds(0, 2)]

        @pl.when(jnp.logical_and(j == stretch * (4 + 2 * depth_of(1)), v != 1))
        def _():
            corner_copy(ext_c, 0).wait_recv()
            corner_forward(ext_c)

        compute(j)

    @pl.loop(n, n + 8 * stretch)
    def _(j):
        side_turns(j)
        compute(j)

    panels.finish_upper()
    panels.finish()

    @pl.loop(0, n)
    def _(j):
        for k in range(2):
            left = goes_up(k)
            if k == 0:
                left = jnp.logical_and(left, jnp.logical_or(z != 1, j >= n - WINDOW))

            @pl.when(left)
            def _():
                up(k, j).wait_send()

            @pl.when(goes_down(k))
            def _():
                down(k, j).wait_send()

            sib(k, j).wait_send()

    @pl.loop(0, ns)
    def _(j):
        for s in range(2):
            for bi in range(nbits):
                @pl.when(label(s) % (2 << bi) == 0)
                def _():
                    side_copy(s, j, bi).wait_send()

    @pl.when(goes_up(1))
    def _():
        ext_copy(ext_r.at[core], 0, other, 3).wait_send()

    @pl.when(goes_down(1))
    def _():
        ext_copy(ext_r.at[core], 1, other, 3).wait_send()

    ext_copy(ext_r.at[core], 2, other, 4).wait_send()
    for bi in range(nbits):
        @pl.when(label(1) % (2 << bi) == 0)
        def _():
            corner_copy(ext_c, bi).wait_send()


def dot(a, b):
    return jnp.dot(a, b, preferred_element_type=jnp.float32)


class Panels:
    def __init__(self, cols, order, inverse, rows, side, ext_r, ext_c, tiles, out, mix, both, final, place):
        self.cols, self.order, self.inverse = cols, order, inverse
        self.rows, self.side, self.ext_r, self.ext_c = rows, side, ext_r, ext_c
        self.tiles, self.out, self.place = tiles, out, place
        self.mix, self.both, self.final = mix, both, final
        self.p = lax.axis_index("prow")
        self.v = lax.axis_index("pcol")

    def prepare(self, mixed, perm):
        spread = lax.broadcasted_iota(jnp.int32, (256, 256), 0)
        for k in range(2):
            turned = jnp.where(self.order[pl.ds(k, 1), :] == spread, 1.0, 0.0)
            perm[k] = turned.T.astype(jnp.bfloat16)
            mixed[k] = dot(self.inverse[k], perm[k]).astype(jnp.bfloat16)
        self.mixed = mixed
        self.perm = perm

    def side_step(self, i, step):
        bf = jnp.bfloat16
        ext_c, side, final, cols = self.ext_c, self.side, self.final, self.cols
        corner = jnp.concatenate(
            [jnp.concatenate([ext_c[0, r], ext_c[1, r]], axis=1) for r in range(2)], axis=0)

        def wide(s):
            return jnp.concatenate(
                [side[s, pl.ds(i, step), h].reshape(step * 128, 128) for h in range(2)], axis=1)

        left = wide(0)
        lower = dot(left, self.mixed[0]).astype(bf)
        self.mix[pl.ds(i, step), :, pl.ds(0, 256)] = lower.reshape(step, 128, 256)
        right = (wide(1).astype(jnp.float32) - dot(lower, corner)).astype(bf)
        self.mix[pl.ds(i, step), :, pl.ds(256, 256)] = dot(right, self.mixed[1]).astype(bf).reshape(step, 128, 256)

        def keep(value):
            for u in range(step):
                for h in range(2):
                    final[cols + 2 * (i + u) + h] = value[u * 128:(u + 1) * 128, h * 128:(h + 1) * 128]

        @pl.when(self.v == 0)
        def _():
            keep(dot(left, self.inverse[0]).astype(bf))

        @pl.when(self.v == 1)
        def _():
            keep(dot(right, self.inverse[1]).astype(bf))

    def pivot_rows(self):
        ext_r = self.ext_r
        return jnp.concatenate(
            [jnp.concatenate([ext_r[r, 0], ext_r[r, 1]], axis=1) for r in range(2)], axis=0)

    def set_lead(self):
        self.lead[...] = dot(self.pivot_rows(), self.mixed[0]).astype(jnp.bfloat16)

    def stacked(self, c, step, half):
        return jnp.concatenate(
            [self.rows[c + u, pl.ds(2 * half, 2)].reshape(256, 128) for u in range(step)], axis=1)

    def row_step(self, c, step):
        top = self.stacked(c, step, 0)
        low = self.stacked(c, step, 1)
        value = (low.astype(jnp.float32) - dot(self.lead[...], top)).astype(jnp.bfloat16)
        for u in range(step):
            self.both[c + u, pl.ds(0, 256)] = top[:, u * 128:(u + 1) * 128]
            self.both[c + u, pl.ds(256, 256)] = value[:, u * 128:(u + 1) * 128]

    def finish_upper(self):
        bf = jnp.bfloat16
        p, both, final, cols = self.p, self.both, self.final, self.cols
        step = 4

        @pl.when(self.v == 0)
        def _():
            value = dot(self.pivot_rows(), self.inverse[0]).astype(bf)
            both[0, pl.ds(256, 256)] = value[:, :128]
            both[1, pl.ds(256, 256)] = value[:, 128:]

        @pl.when(p < 2)
        def _():
            part = self.perm[0, pl.ds(p * 128, 128)]

            @pl.loop(0, cols, step=step)
            def _(c):
                value = dot(part, self.stacked(c, step, 0)).astype(bf)
                for u in range(step):
                    final[c + u] = value[:, u * 128:(u + 1) * 128]

        @pl.when(jnp.logical_and(p >= 2, p < 4))
        def _():
            part = self.perm[1, pl.ds((p - 2) * 128, 128)]

            @pl.loop(0, cols, step=step)
            def _(c):
                low = jnp.concatenate([both[c + u, pl.ds(256, 256)] for u in range(step)], axis=1)
                value = dot(part, low).astype(bf)
                for u in range(step):
                    final[c + u] = value[:, u * 128:(u + 1) * 128]

    def finish(self):
        place, tiles, final = self.place, self.tiles, self.final

        @pl.loop(0, tiles.shape[0], step=GROUP)
        def _(base):
            for u in range(GROUP):
                s = base + u
                i, c, f, kind = place[0, s], place[1, s], place[2, s], place[3, s]
                base_value = jnp.where(kind == 1, final[f], tiles[s]).astype(jnp.float32)
                total = dot(self.mix[i], self.both[c])
                self.out[s] = (base_value - jnp.where(kind == 0, 1.0, 0.0) * total).astype(jnp.bfloat16)


def local(tiles, tile_pos, pivots, inverses):
    slots, edge, _ = tiles.shape
    row_procs = lax.axis_size("prow")
    col_procs = lax.axis_size("pcol")
    nz = row_procs // 2
    nbits = col_procs.bit_length() - 1
    cols = ROW_TILES * row_procs // col_procs
    tile_row = tile_pos[:, 0]
    tile_col = tile_pos[:, 1]
    local_row = jnp.clip(tile_row // row_procs, 0, ROW_TILES - 1)
    local_col = jnp.clip(2 * (tile_col // 2 // col_procs) + tile_col % 2, 0, cols - 1)
    listed = tile_row >= 0
    is_upper = listed & (tile_row < 4)
    is_side = listed & (tile_col < 4)
    side_key = local_row * 2 + tile_col % 2
    targets = jnp.arange(cols + 2 * ROW_TILES, dtype=jnp.int32)[:, None]
    upper_key = jnp.where(is_upper, local_col, -1)[None, :]
    lower_key = jnp.where(is_side, cols + side_key, -1)[None, :]
    match = jnp.where(targets < cols, upper_key, lower_key) == targets
    found = jnp.sum(jnp.where(match, jnp.arange(slots, dtype=jnp.int32)[None, :], 0), axis=1)
    done = jnp.where(is_upper, local_col, cols + side_key)
    kind = jnp.where(listed, jnp.where(is_upper | is_side, 1, 0), 2)
    done = jnp.where(kind == 1, done, 0)
    place = jnp.stack([local_row, local_col, done, kind]).astype(jnp.int32)

    bf = jnp.bfloat16
    smem = pl.BlockSpec(memory_space=pltpu.SMEM)
    vmem = pl.BlockSpec(memory_space=pltpu.VMEM)
    dma = pltpu.SemaphoreType.DMA
    n = CHUNKS
    panel = 2 * edge
    return pl.pallas_call(
        functools.partial(exchange, nz, nbits, cols),
        out_shape=jax.ShapeDtypeStruct(tiles.shape, bf),
        in_specs=[smem, smem, vmem, pl.BlockSpec(memory_space=pl.ANY), pl.BlockSpec(memory_space=pl.ANY)],
        out_specs=vmem,
        scratch_shapes=[
            pltpu.VMEM(tiles.shape, bf),
            pltpu.VMEM((2, panel, panel), bf),
            pltpu.VMEM((2, panel, panel), bf),
            pltpu.VMEM((cols, 4, edge, edge), bf),
            pltpu.VMEM((2, ROW_TILES, 2, edge, edge), bf),
            pltpu.VMEM((2, 2, edge, edge), bf),
            pltpu.VMEM((2, 2, edge, edge), bf),
            pltpu.VMEM((ROW_TILES, edge, 2 * panel), bf),
            pltpu.VMEM((cols, 2 * panel, edge), bf),
            pltpu.VMEM((cols + 2 * ROW_TILES, edge, edge), bf),
            pltpu.VMEM((2, panel, panel), bf),
            pltpu.VMEM((panel, panel), bf),
            dma((2, n)), dma((2, n)), dma((2, n)), dma((2, n)), dma((2, n)),
            dma((2, nbits, SIDE_CHUNKS)), dma((2, SIDE_CHUNKS)), dma((5,)), dma((nbits,)), dma((1,)), dma((2,)),
        ],
        compiler_params=pltpu.CompilerParams(
            collective_id=0, has_side_effects=True, vmem_limit_bytes=48 * 1024 * 1024),
        name="exchange",
    )(found, place, pivots, inverses, tiles)


def solution(mesh):
    return jax.shard_map(
        local,
        mesh=mesh,
        in_specs=(P(("prow", "pcol"), None, None), P(("prow", "pcol"), None), P(), P()),
        out_specs=P(("prow", "pcol"), None, None),
        check_vma=False,
    )
```
